32 devices in a mesh: dp: 4 (over y, core), tensor: 8 (over z, x).
Axes of the slice: x: 2, y: 2, z: 4, core: 2. Of those that a mesh axis runs over, the one named last changes fastest.
Arguments:
- hidden_sel: bfloat16 [4, 512, 2048], P('dp', 'tensor'), may hold values from -8 to 8
- picked: int32 [4, 512], P('dp'), may hold values from 0 to 12287, as said below
- order: int32 [4, 12], P('dp'), may hold values from 0 to 11, each once within a row
- lengths: int32 [4, 3], P('dp'), may hold values from 1 to 6, 12 in all within a row
- offsets: int32 [4, 3], P('dp'), may hold values from 0 to 4095
- cache_keys: bfloat16 [4, 12288, 2048], P('dp', 'tensor'), may hold values from -64 to 64
- cache_values: bfloat16 [4, 12288, 2048], P('dp', 'tensor'), may hold values from -6 to 6
- w_qkv: bfloat16 [3, 2048, 2048], P(None, 'dp', 'tensor'), may hold values from -0.088388348 to 0.088388348
- w_out: bfloat16 [2048, 2048], P('tensor', 'dp'), may hold values from -0.125 to 0.125
- w_gate_up: bfloat16 [2, 2048, 8192], P(None, 'dp', 'tensor'), may hold values from -0.125 to 0.125
- w_down: bfloat16 [8192, 2048], P('tensor', 'dp'), may hold values from -0.0625 to 0.0625
- gains: float32 [4, 2048], replicated, may hold values from 0.5 to 1.5
Outputs:
- layer_out: bfloat16 [4, 512, 2048], P('dp', 'tensor')
- fresh_keys: bfloat16 [4, 512, 2048], P('dp', 'tensor')
The draws below stay inside these ranges and needn't reach their ends.
Inputs may be any that keep to these rules, and one draw needn't show every extreme that they name: `picked`: distinct context rows in increasing order; the first and last rows of the context are always among them. `lengths`: they sum to 12.
All inputs are finite; a program needn't handle non-finite values.
Results may differ from the reference program's by a relative error of at most 0.04.
Values may be sent and summed in bfloat16 or wider, within the bound.
No kernel may reach another device: no remote copies, remote signals or barrier semaphores. Data moves between devices by JAX's collectives and lax.ppermute only.
A program may use at most 128 MiB of HBM per device.

```python
import math
import jax
import jax.numpy as jnp
import numpy as np
from jax import lax

D = 2048
HEADS = 16
HEAD_DIM = 128
FF = 8192
CH = 1024
NCH = 12
REQS = 3
SEL = 512
CTX = 12288
GROUPS = 4
N_TENSOR = 8


def draw_picked(key, part):

    def one_group(group_key):
        inner = jax.random.permutation(group_key, CTX - 2)[:SEL - 2].astype(jnp.int32) + 1
        return jnp.concatenate([jnp.zeros((1,), jnp.int32), jnp.sort(inner).astype(jnp.int32), jnp.full((1,), CTX - 1, jnp.int32)])
    group_keys = jax.random.split(jax.random.fold_in(key, 7), GROUPS)
    return jax.vmap(one_group)(group_keys)


def projection_block(key):
    return jax.random.truncated_normal(jax.random.fold_in(key, 101), -4.0, 4.0, (3, D, D), jnp.float32) * D ** (-0.5)


def aligned_features(key):
    quarter = max(2, HEAD_DIM // 16)
    chosen_head = jax.random.randint(jax.random.fold_in(key, 103), (), 0, HEADS).astype(jnp.int32)
    within = jnp.concatenate([jnp.arange(HEAD_DIM // 2 - quarter, HEAD_DIM // 2, dtype=jnp.int32), jnp.arange(HEAD_DIM - quarter, HEAD_DIM, dtype=jnp.int32)])
    features = chosen_head * HEAD_DIM + within
    sign_pattern = jnp.where(jax.random.bernoulli(jax.random.fold_in(key, 104), 0.5, (2 * quarter,)), 1.0, -1.0).astype(jnp.float32)
    return (features, sign_pattern)


def draw_w_qkv(key, part):
    return projection_block(key).astype(jnp.bfloat16)


def draw_hidden_sel(key, part):
    noise_rows = jax.random.truncated_normal(jax.random.fold_in(key, 105), -6.0, 6.0, (GROUPS, SEL, D), jnp.float32)
    weights_query = projection_block(key)[0]
    features, sign_pattern = aligned_features(key)
    picked_columns = jnp.take(weights_query, features, axis=1)
    direction = picked_columns[:, 0] * sign_pattern[0]
    for column in range(1, sign_pattern.shape[0]):
        direction = direction + picked_columns[:, column] * sign_pattern[column]
    aligned_rows = jax.random.bernoulli(jax.random.fold_in(key, 116), 0.1, (GROUPS, SEL))
    strength = jax.random.uniform(jax.random.fold_in(key, 117), (GROUPS, SEL), jnp.float32, 10.0, 18.0)
    lift_rows = jnp.where(aligned_rows, strength, 0.0)
    noise_rows = jnp.clip(noise_rows + lift_rows[:, :, None] * direction[None, None, :], -8.0, 8.0)
    return noise_rows.astype(jnp.bfloat16)


def draw_cache_keys(key, part):
    base_keys = jax.random.truncated_normal(jax.random.fold_in(key, 108), -6.0, 6.0, (GROUPS, CTX, D), jnp.float32)
    features, sign_pattern = aligned_features(key)
    band_rows = jax.random.bernoulli(jax.random.fold_in(key, 119), 0.05, (GROUPS, CTX))
    strength = jax.random.uniform(jax.random.fold_in(key, 120), (GROUPS, CTX), jnp.float32, 30.0, 55.0)
    current = base_keys[:, :, features]
    lifted = jnp.where(band_rows[:, :, None], strength[:, :, None] * sign_pattern[None, None, :], current)
    base_keys = base_keys.at[:, :, features].set(lifted)
    return base_keys.astype(jnp.bfloat16)


def with_ends(values, rng, smallest, largest):
    longest = values.shape.index(max(values.shape))
    spots = []
    for shift in (0, 1):
        where = [jax.random.randint(jax.random.fold_in(rng, axis), (), 0, length) for axis, length in enumerate(values.shape)]
        where[longest] = (where[longest] + shift) % values.shape[longest]
        spots.append(tuple(where))
    return values.at[spots[0]].set(smallest).at[spots[1]].set(largest)


def shard_levels(rng, extent, shards, least, high):
    level = 1.0
    for axis_at, shards_of in shards:
        heights = jax.random.uniform(jax.random.fold_in(jax.random.fold_in(rng, 6), axis_at), (shards_of,), jnp.float32, least / len(shards), high / len(shards))
        level = level * jnp.repeat(jnp.exp(heights), extent[axis_at] // shards_of).reshape((-1,) + (1,) * (len(extent) - 1 - axis_at))
    return level


def split_up(number_of, total, reach, slope):
    loads = [(1 << 20) // math.isqrt(rank ** slope) + 1 for rank in range(2, number_of + 1)]
    surplus, counts = total - reach - (number_of - 1), [1] * (number_of - 1)
    while surplus > 0:
        movable = [i for i in range(number_of - 1) if counts[i] < reach]
        whole, remaining = sum([loads[i] for i in movable]), surplus
        for i in movable:
            extra = min(reach - counts[i], max(1, remaining * loads[i] // whole), surplus)
            counts[i] = counts[i] + extra
            surplus = surplus - extra
    return np.array([reach] + counts)


def uneven(stream_key, number_of, total, reach, skew):
    if number_of == 2:
        one = jax.random.randint(stream_key, (), max(1, total - reach), min(reach, total - 1) + 1)
        return jnp.stack([one, total - one])
    sizes = jnp.asarray(split_up(number_of, total, reach, skew), jnp.int32)
    couples = (number_of - 1) // 2
    donor, receiver = sizes[1:1 + 2 * couples:2], sizes[2:2 + 2 * couples:2]
    slack = jnp.minimum(donor - 1, reach - receiver)
    passed = jax.random.randint(jax.random.fold_in(stream_key, 1), (couples,), 0, 1 << 20) % (slack + 1)
    sizes = sizes.at[1:1 + 2 * couples:2].set(donor - passed).at[2:2 + 2 * couples:2].set(receiver + passed)
    return sizes[jax.random.permutation(jax.random.fold_in(stream_key, 2), number_of)]


def normal_values(rng, dims, deviation, most, cuts=(), kind=jnp.bfloat16):
    entries = deviation * jax.random.normal(rng, dims, jnp.float32)
    if cuts:
        entries = entries * shard_levels(rng, dims, cuts, -0.22, 0.18)
    return jnp.clip(entries, -most, most).astype(kind)


def setup_inputs(seed: int = 0) -> dict:
    streams_of = jax.random.split(jax.random.key(seed), 13)
    return {
        "hidden_sel": draw_hidden_sel(jax.random.fold_in(streams_of[12], 71), 0),
        "picked": draw_picked(jax.random.fold_in(streams_of[12], 71), 0),
        "order": jax.vmap(lambda own: jax.random.permutation(own, NCH))(jax.random.split(streams_of[2], GROUPS)).reshape((GROUPS, NCH)).astype(jnp.int32),
        "lengths": jax.vmap(lambda own: uneven(own, REQS, NCH, NCH // 2, 2))(jax.random.split(streams_of[3], GROUPS)).reshape((GROUPS, REQS)).astype(jnp.int32),
        "offsets": with_ends(jax.random.randint(streams_of[4], (GROUPS, REQS), 0, 4096), jax.random.fold_in(streams_of[4], 1), 0, 4095).astype(jnp.int32),
        "cache_keys": draw_cache_keys(jax.random.fold_in(streams_of[12], 71), 0),
        "cache_values": normal_values(streams_of[6], (GROUPS, CTX, D), 1.0, 6.0, ((0, 4), (1, 8))),
        "w_qkv": draw_w_qkv(jax.random.fold_in(streams_of[12], 71), 0),
        "w_out": normal_values(streams_of[8], (D, D), D ** -0.5, 0.125, ((0, 8), (1, 4))),
        "w_gate_up": normal_values(streams_of[9], (2, D, FF), D ** -0.5, 0.125, ((1, 4), (2, 8))),
        "w_down": normal_values(streams_of[10], (FF, D), FF ** -0.5, 0.0625, ((0, 8), (1, 4))),
        "gains": jnp.clip(1.0 + 0.1 * jax.random.normal(streams_of[11], (4, D), jnp.float32), 0.5, 1.5),
    }


THETA = 500000.0
EPSILON = 1e-06
NEGATIVE = -1e+30

def token_meta(rows, order_row, length_row, offset_row):
    slot_index = rows // CH
    in_span = rows % CH
    ordinal = lax.optimization_barrier(jnp.sum(jnp.where(slot_index[:, None] == jnp.arange(NCH, dtype=jnp.int32)[None, :], order_row[None, :], 0), axis=1))
    request_end = jnp.cumsum(length_row).astype(jnp.int32)
    request = lax.optimization_barrier(jnp.sum((ordinal[:, None] >= request_end[None, :]).astype(jnp.int32), axis=1))
    request_pick = request[:, None] == jnp.arange(REQS, dtype=jnp.int32)[None, :]
    request_start = lax.optimization_barrier(jnp.sum(jnp.where(request_pick, (request_end - length_row)[None, :], 0), axis=1))
    request_shift = lax.optimization_barrier(jnp.sum(jnp.where(request_pick, offset_row[None, :], 0), axis=1))
    position = request_shift + (ordinal - request_start) * CH + in_span
    return (request, position, in_span)

def frequencies(index_float):
    return jnp.exp(index_float * (-2.0 * math.log(THETA) / HEAD_DIM))

def rope_full(values_in, position):
    row_count = values_in.shape[0]
    half_dim = HEAD_DIM // 2
    split = values_in.reshape(row_count, -1, HEAD_DIM)
    angles = position.astype(jnp.float32)[:, None] * frequencies(jnp.arange(half_dim, dtype=jnp.int32).astype(jnp.float32))[None, :]
    cosine = jnp.cos(angles)[:, None, :]
    sine = jnp.sin(angles)[:, None, :]
    first = split[..., :half_dim]
    second = split[..., half_dim:]
    turned = jnp.concatenate([first * cosine - second * sine, second * cosine + first * sine], axis=-1)
    return turned.reshape(row_count, -1)

def rms_scale(values_in, gain):
    return values_in * lax.rsqrt(lax.optimization_barrier(jnp.mean(values_in * values_in, axis=-1, keepdims=True)) + EPSILON) * gain

def blocked_product(left, right, blocks):
    row_count, inner = left.shape
    left_blocks = left.reshape(row_count, blocks, inner // blocks).transpose(1, 0, 2)
    right_blocks = right.reshape(blocks, inner // blocks, right.shape[1])

    def step(totals, pair):
        part = jnp.dot(pair[0], pair[1], preferred_element_type=jnp.float32)
        part = lax.optimization_barrier(part.astype(jnp.bfloat16)).astype(jnp.float32)
        return (totals + part, None)
    start = jnp.zeros((row_count, right.shape[1]), jnp.float32)
    totals, _ = lax.scan(step, start, (left_blocks, right_blocks))
    return totals

def one_group(hidden, picked_row, order_row, length_row, offset_row, keys_cached, values_cached, w_qkv, w_out, w_gate_up, w_down, gains):
    context_rows = jnp.arange(CTX, dtype=jnp.int32)
    key_request, key_position, key_local = token_meta(context_rows, order_row, length_row, offset_row)
    query_request, query_position, _ = token_meta(picked_row, order_row, length_row, offset_row)
    chosen = jnp.zeros((CTX,), jnp.int32).at[picked_row].set(1)
    projected = jnp.einsum('nd,kdc->knc', hidden.astype(jnp.float32), w_qkv.astype(jnp.float32))
    query = rope_full(rms_scale(projected[0], gains[0]), query_position).astype(jnp.bfloat16)
    fresh_keys = rope_full(rms_scale(projected[1], gains[1]), query_position).astype(jnp.bfloat16)
    fresh_values = projected[2].astype(jnp.bfloat16)
    turned = rope_full(keys_cached.astype(jnp.float32), key_position - key_local).astype(jnp.bfloat16)
    usable_cached = (query_request[:, None] == key_request[None, :]) & (key_position[None, :] <= query_position[:, None]) & (chosen[None, :] == 0)
    usable_fresh = (query_request[:, None] == query_request[None, :]) & (query_position[None, :] <= query_position[:, None])
    usable_c = usable_cached.reshape(SEL, N_TENSOR, -1)
    usable_f = usable_fresh.reshape(SEL, N_TENSOR, -1)

    def per_head(operands):
        query_h, key_c, value_c, key_f, value_f = operands
        scores_c = jnp.dot(query_h, key_c.T, preferred_element_type=jnp.float32) * HEAD_DIM ** (-0.5)
        scores_f = jnp.dot(query_h, key_f.T, preferred_element_type=jnp.float32) * HEAD_DIM ** (-0.5)
        masked_c = jnp.where(usable_cached, scores_c, NEGATIVE).reshape(SEL, N_TENSOR, -1)
        masked_f = jnp.where(usable_fresh, scores_f, NEGATIVE).reshape(SEL, N_TENSOR, -1)
        block_max = jnp.maximum(lax.optimization_barrier(jnp.max(masked_c, axis=2)), lax.optimization_barrier(jnp.max(masked_f, axis=2)))
        expo_c = jnp.where(usable_c, jnp.exp(masked_c - block_max[:, :, None]), 0.0)
        expo_f = jnp.where(usable_f, jnp.exp(masked_f - block_max[:, :, None]), 0.0)
        totals = lax.optimization_barrier(jnp.sum(expo_c, axis=2)) + lax.optimization_barrier(jnp.sum(expo_f, axis=2))
        weight_c = lax.optimization_barrier(expo_c.astype(jnp.bfloat16)).astype(jnp.float32)
        weight_f = lax.optimization_barrier(expo_f.astype(jnp.bfloat16)).astype(jnp.float32)
        mixed = jnp.einsum('qtk,tkd->qtd', weight_c, value_c.reshape(N_TENSOR, -1, HEAD_DIM).astype(jnp.float32))
        mixed = mixed + jnp.einsum('qtk,tkd->qtd', weight_f, value_f.reshape(N_TENSOR, -1, HEAD_DIM).astype(jnp.float32))
        overall = lax.optimization_barrier(jnp.max(block_max, axis=1))
        factor = jnp.exp(block_max - overall[:, None])
        parts = lax.optimization_barrier((mixed * factor[:, :, None]).astype(jnp.bfloat16)).astype(jnp.float32)
        return lax.optimization_barrier(jnp.sum(parts, axis=1)) / lax.optimization_barrier(jnp.sum(totals * factor, axis=1))[:, None]

    def by_head(array_in):
        return array_in.reshape(array_in.shape[0], HEADS, HEAD_DIM).transpose(1, 0, 2)
    heads_out = lax.map(per_head, (by_head(query), by_head(turned), by_head(values_cached), by_head(fresh_keys), by_head(fresh_values)))
    attn = heads_out.transpose(1, 0, 2).reshape(SEL, D).astype(jnp.bfloat16)
    y_out = blocked_product(attn, w_out, N_TENSOR)
    hidden_next = (hidden.astype(jnp.float32) + rms_scale(y_out, gains[2])).astype(jnp.bfloat16)
    gate_part = jnp.dot(hidden_next, w_gate_up[0], preferred_element_type=jnp.float32)
    up_part = jnp.dot(hidden_next, w_gate_up[1], preferred_element_type=jnp.float32)
    activated = (jax.nn.silu(gate_part) * up_part).astype(jnp.bfloat16)
    z_out = blocked_product(activated, w_down, N_TENSOR)
    layer_out = (hidden_next.astype(jnp.float32) + rms_scale(z_out, gains[3])).astype(jnp.bfloat16)
    return (layer_out, fresh_keys)

def reference(hidden_sel, picked, order, lengths, offsets, cache_keys, cache_values, w_qkv, w_out, w_gate_up, w_down, gains):
    outputs = []
    keys_out = []
    for group in range(GROUPS):
        layer_out, fresh_keys = one_group(hidden_sel[group], picked[group], order[group], lengths[group], offsets[group], cache_keys[group], cache_values[group], w_qkv, w_out, w_gate_up, w_down, gains)
        outputs.append(layer_out)
        keys_out.append(fresh_keys)
    return (jnp.stack(outputs), jnp.stack(keys_out))
```

```python
import functools
import math

import jax
import jax.numpy as jnp
from jax import lax
from jax.experimental import pallas as pl
from jax.experimental.pallas import tpu as pltpu
from jax.sharding import PartitionSpec as P

HEAD_DIM = 128
CH = 1024
NCH = 12
REQS = 3


THETA = 500000.0
EPSILON = 1e-06
NEGATIVE = -1e30
FLOOR = -1e28
VMEM_BYTES = 48 * 1024 * 1024


def token_meta(rows, order_row, length_row, offset_row):
    slot_index = rows // CH
    in_span = rows % CH
    ordinal = jnp.sum(
        jnp.where(
            slot_index[:, None] == jnp.arange(NCH, dtype=jnp.int32)[None, :], order_row[None, :], 0
        ),
        axis=1,
    )
    request_end = jnp.cumsum(length_row)
    request = jnp.sum((ordinal[:, None] >= request_end[None, :]).astype(jnp.int32), axis=1)
    request_pick = request[:, None] == jnp.arange(REQS, dtype=jnp.int32)[None, :]
    request_start = jnp.sum(jnp.where(request_pick, (request_end - length_row)[None, :], 0), axis=1)
    request_shift = jnp.sum(jnp.where(request_pick, offset_row[None, :], 0), axis=1)
    position = request_shift + (ordinal - request_start) * CH + in_span
    return (request, position, in_span)


def frequencies(index_float):
    return jnp.exp(index_float * (-2.0 * math.log(THETA) / HEAD_DIM))


def rope_full(values_in, position):
    row_count = values_in.shape[0]
    half_dim = HEAD_DIM // 2
    split = values_in.reshape(row_count, -1, HEAD_DIM)
    angles = (
        position.astype(jnp.float32)[:, None]
        * frequencies(jnp.arange(half_dim, dtype=jnp.int32).astype(jnp.float32))[None, :]
    )
    cosine = jnp.cos(angles)[:, None, :]
    sine = jnp.sin(angles)[:, None, :]
    first = split[..., :half_dim]
    second = split[..., half_dim:]
    turned = jnp.concatenate(
        [first * cosine - second * sine, second * cosine + first * sine], axis=-1
    )
    return turned.reshape(row_count, -1)


def rms_scale(values_in, gain):
    return (
        values_in
        * lax.rsqrt(jnp.mean(values_in * values_in, axis=-1, keepdims=True) + EPSILON)
        * gain
    )


def shards(
    hidden_sel,
    picked,
    order,
    lengths,
    offsets,
    cache_keys,
    cache_values,
    w_qkv,
    w_out,
    w_gate_up,
    w_down,
    gains,
):
    hidden = hidden_sel[0]
    picked_row = picked[0]
    order_row = order[0]
    length_row = lengths[0]
    offset_row = offsets[0]
    keys_local = cache_keys[0]
    values_local = cache_values[0]
    lane_count = lax.axis_size("tensor")
    lane_index = lax.axis_index("tensor")
    sel_dev = hidden.shape[0]
    sel_all = sel_dev * lane_count
    ctx_dev = keys_local.shape[0]
    model_width = hidden.shape[1]
    head_count = model_width // HEAD_DIM
    qkv_full, out_full = (
        lax.all_gather(w_qkv, "dp", axis=1, tiled=True),
        lax.all_gather(w_out, "dp", axis=1, tiled=True),
    )
    query_request, query_position, _ = token_meta(picked_row, order_row, length_row, offset_row)
    cache_rows = lane_index * ctx_dev + jnp.arange(ctx_dev, dtype=jnp.int32)
    cache_request, cache_position, cache_local = token_meta(
        cache_rows, order_row, length_row, offset_row
    )
    chosen = jnp.any(picked_row[:, None] == cache_rows[None, :], axis=0)
    fresh_request = lax.dynamic_slice_in_dim(query_request, lane_index * sel_dev, sel_dev)
    fresh_position = lax.dynamic_slice_in_dim(query_position, lane_index * sel_dev, sel_dev)
    projected = jnp.einsum(
        "nd,kdc->knc",
        lax.all_gather(hidden, "tensor", axis=0, tiled=True),
        qkv_full,
        preferred_element_type=jnp.float32,
    )
    own_rows = lax.all_to_all(
        projected.astype(jnp.bfloat16), "tensor", split_axis=1, concat_axis=2, tiled=True
    ).astype(projected.dtype)
    query_tok = rope_full(rms_scale(own_rows[0], gains[0]), fresh_position).astype(jnp.bfloat16)
    key_fresh = rope_full(rms_scale(own_rows[1], gains[1]), fresh_position).astype(jnp.bfloat16)
    value_fresh = own_rows[2].astype(jnp.bfloat16)
    queries = lax.all_gather(query_tok, "tensor", axis=0, tiled=True)
    turned_keys = rope_full(keys_local.astype(jnp.float32), cache_position - cache_local).astype(
        jnp.bfloat16
    )
    all_keys = jnp.concatenate([turned_keys, key_fresh], axis=0).reshape(-1, head_count, HEAD_DIM)
    all_values = jnp.concatenate([values_local, value_fresh], axis=0).reshape(
        -1, head_count, HEAD_DIM
    )
    key_request = jnp.concatenate([cache_request, fresh_request])
    key_position = jnp.concatenate([cache_position, fresh_position])
    key_live = jnp.concatenate([jnp.logical_not(chosen), jnp.ones((sel_dev,), bool)])
    block_rows = min(512, sel_all)
    block_count = sel_all // block_rows

    def attend(operands):
        query_block, block_request, block_position = operands
        scores = jnp.einsum(
            "qhd,khd->hqk",
            query_block.reshape(block_rows, head_count, HEAD_DIM),
            all_keys,
            preferred_element_type=jnp.float32,
        ) * HEAD_DIM ** (-0.5)
        usable = (
            (block_request[:, None] == key_request[None, :])
            & (key_position[None, :] <= block_position[:, None])
            & key_live[None, :]
        )
        masked = jnp.where(usable[None], scores, NEGATIVE)
        local_max = jnp.max(masked, axis=2)
        weights = jnp.where(usable[None], jnp.exp(masked - local_max[:, :, None]), 0.0)
        totals = jnp.sum(weights, axis=2)
        mixed = jnp.einsum(
            "hqk,khd->qhd",
            weights.astype(jnp.bfloat16),
            all_values,
            preferred_element_type=jnp.float32,
        )
        return (mixed.reshape(block_rows, model_width), local_max.T, totals.T)

    partial_out, local_max, totals = lax.map(
        attend,
        (
            queries.reshape(block_count, block_rows, model_width),
            query_request.reshape(block_count, block_rows),
            query_position.reshape(block_count, block_rows),
        ),
    )
    partial_out = partial_out.reshape(sel_all, model_width)
    local_max = local_max.reshape(sel_all, head_count)
    totals = totals.reshape(sel_all, head_count)
    row_max = lax.pmax(local_max.astype(jnp.bfloat16), "tensor").astype(local_max.dtype)
    factor = jnp.exp(local_max - row_max)
    scaled_out = (partial_out.reshape(sel_all, head_count, HEAD_DIM) * factor[:, :, None]).reshape(
        sel_all, model_width
    )
    scaled_total = totals * factor
    summed = lax.psum_scatter(
        scaled_out.astype(jnp.bfloat16), "tensor", scatter_dimension=0, tiled=True
    ).astype(jnp.float32)
    weight_sum = lax.psum_scatter(
        scaled_total.astype(jnp.bfloat16), "tensor", scatter_dimension=0, tiled=True
    ).astype(jnp.float32)
    attn_rows = (
        (summed.reshape(sel_dev, head_count, HEAD_DIM) / weight_sum[:, :, None])
        .reshape(sel_dev, model_width)
        .astype(jnp.bfloat16)
    )
    attn_cols = lax.all_to_all(attn_rows, "tensor", split_axis=1, concat_axis=0, tiled=True)
    attn_proj = lax.psum_scatter(
        jnp.dot(attn_cols, out_full, preferred_element_type=jnp.float32).astype(jnp.bfloat16),
        "tensor",
        scatter_dimension=0,
        tiled=True,
    ).astype(jnp.float32)
    hidden_next = (hidden.astype(jnp.float32) + rms_scale(attn_proj, gains[2])).astype(jnp.bfloat16)
    gate_full, down_full = (
        lax.all_gather(w_gate_up, "dp", axis=1, tiled=True),
        lax.all_gather(w_down, "dp", axis=1, tiled=True),
    )
    rows_piece = lax.all_gather(hidden_next, "tensor", axis=0, tiled=True)
    gate_part = jnp.dot(rows_piece, gate_full[0], preferred_element_type=jnp.float32)
    up_part = jnp.dot(rows_piece, gate_full[1], preferred_element_type=jnp.float32)
    activated = (jax.nn.silu(gate_part) * up_part).astype(jnp.bfloat16)
    mlp_out = lax.psum_scatter(
        jnp.dot(activated, down_full, preferred_element_type=jnp.float32).astype(jnp.bfloat16),
        "tensor",
        scatter_dimension=0,
        tiled=True,
    ).astype(jnp.float32)
    result = (hidden_next.astype(jnp.float32) + rms_scale(mlp_out, gains[3])).astype(jnp.bfloat16)
    return (result[None], key_fresh[None])


def lane_at(place, count):
    place = place % count
    return jnp.where(place < count // 2, 2 * place, 2 * (count - place) - 1)


def ring_steps(count, shift):
    around = list(range(0, count, 2)) + list(range(count - 1, 0, -2))
    return [(around[i], around[(i + shift) % count]) for i in range(count)]


def ring_gather(block, count):
    blocks = [block] + [None] * (count - 1)
    forth = back = block
    for step in range(1, count // 2 + 1):
        forth = lax.ppermute(forth, "tensor", ring_steps(count, 1))
        blocks[step] = forth
        if step < count - step:
            back = lax.ppermute(back, "tensor", ring_steps(count, -1))
            blocks[count - step] = back
    return blocks


def ring_scatter(pieces, count, merge):
    back = pieces[count // 2]
    forth = pieces[count // 2 + 1]
    for step in range(count // 2, 0, -1):
        back = lax.ppermute(back, "tensor", ring_steps(count, -1))
        if step > 1:
            back = merge(back, pieces[step - 1])
        if step > 1:
            forth = lax.ppermute(forth, "tensor", ring_steps(count, 1))
            if step > 2:
                forth = merge(forth, pieces[count - step + 2])
    return back, forth


def add_rounded(left, right):
    return (left.astype(jnp.float32) + right.astype(jnp.float32)).astype(jnp.bfloat16)


def dp_shards(weight):
    across = lax.ppermute(weight, "dp", [(i, i ^ 2) for i in range(4)])
    beside = lax.ppermute(weight, "dp", [(i, i ^ 1) for i in range(4)])
    across_beside = lax.ppermute(across, "dp", [(i, i ^ 1) for i in range(4)])
    return [weight, beside, across, across_beside]


def swap_features(values_in, group):
    width = values_in.shape[-1]
    q0, q1, q2, q3 = jnp.split(values_in, 4, axis=-1)
    odd = (group % 2) == 1
    high = (group // 2) == 1
    q0, q1 = jnp.where(odd, q1, q0), jnp.where(odd, q0, q1)
    q2, q3 = jnp.where(odd, q3, q2), jnp.where(odd, q2, q3)
    q0, q2 = jnp.where(high, q2, q0), jnp.where(high, q0, q2)
    q1, q3 = jnp.where(high, q3, q1), jnp.where(high, q1, q3)
    return jnp.concatenate([q0, q1, q2, q3], axis=-1).reshape(values_in.shape[:-1] + (width,))


def turn_kernel(cos_ref, sin_ref, keys_ref, out_ref):
    for head in range(keys_ref.shape[1] // HEAD_DIM):
        cols = slice(head * HEAD_DIM, (head + 1) * HEAD_DIM)
        part = keys_ref[:, cols].astype(jnp.float32)
        turned = part * cos_ref[0] + pltpu.roll(part, HEAD_DIM // 2, 1) * sin_ref[0]
        out_ref[:, cols] = turned.astype(jnp.bfloat16)


def turn_keys(keys, cosine, sine):
    blocks = cosine.shape[0]
    rows, width = keys.shape
    per = rows // blocks
    table = pl.BlockSpec((1, 1, HEAD_DIM), lambda i: (i, 0, 0))
    body = pl.BlockSpec((per, width), lambda i: (i, 0))
    return pl.pallas_call(
        turn_kernel,
        grid=(blocks,),
        in_specs=[table, table, body],
        out_specs=body,
        out_shape=jax.ShapeDtypeStruct(keys.shape, jnp.bfloat16),
        compiler_params=pltpu.CompilerParams(vmem_limit_bytes=VMEM_BYTES),
        cost_estimate=pl.CostEstimate(
            flops=4 * rows * width, bytes_accessed=4 * rows * width, transcendentals=0
        ),
        name="turn_keys",
    )(cosine[:, None, :], sine[:, None, :], keys)


def tail_rows(rows, wide):
    at = lax.broadcasted_iota(jnp.int32, (16, wide), 0)
    tail = jnp.zeros((16, wide), jnp.float32)
    for index, row in enumerate(rows):
        tail = jnp.where(at == index, row, tail)
    return tail.astype(jnp.bfloat16)


def attend_kernel(lanes_ref, q_ref, gain_ref, cos_ref, sin_ref, k_ref, v_ref, bias_ref, out_ref):
    width = q_ref.shape[2]
    heads = width // HEAD_DIM
    queries = q_ref.shape[1]
    wide = min(256, queries)
    for start in range(0, queries, wide):
        rows = slice(start, start + wide)
        bias = bias_ref[:, rows]
        tops, totals = [], []
        for head in range(heads):
            cols = slice(head * HEAD_DIM, (head + 1) * HEAD_DIM)
            raw = q_ref[0, rows, cols].astype(jnp.float32) * gain_ref[0, :, cols]
            query = raw * cos_ref[rows, :] + pltpu.roll(raw, HEAD_DIM // 2, 1) * sin_ref[rows, :]
            scores = lax.dot_general(
                k_ref[:, cols],
                query.astype(jnp.bfloat16),
                (((1,), (1,)), ((), ())),
                preferred_element_type=jnp.float32,
            )
            scores = scores + bias
            top = jnp.maximum(jnp.max(scores, axis=0, keepdims=True), FLOOR)
            top = top.astype(jnp.bfloat16).astype(jnp.float32)
            weights = jnp.exp2(scores - top)
            tops.append(top)
            totals.append(jnp.sum(weights, axis=0, keepdims=True))
            mixed = jnp.dot(
                v_ref[cols, :], weights.astype(jnp.bfloat16), preferred_element_type=jnp.float32
            )
            out_ref[0, cols, rows] = mixed.astype(jnp.bfloat16)
        out_ref[0, width : width + 16, rows] = tail_rows(tops + totals, wide)


def attend(q_blocks, lanes, gain_blocks, cosine, sine, keys, values_t, bias):
    count, queries, width = q_blocks.shape
    key_rows = keys.shape[0]
    grid_spec = pltpu.PrefetchScalarGridSpec(
        num_scalar_prefetch=1,
        grid=(count,),
        in_specs=[
            pl.BlockSpec((1, queries, width), lambda i, lanes: (i, 0, 0)),
            pl.BlockSpec((1, 1, width), lambda i, lanes: (i, 0, 0)),
            pl.BlockSpec((queries, HEAD_DIM), lambda i, lanes: (0, 0)),
            pl.BlockSpec((queries, HEAD_DIM), lambda i, lanes: (0, 0)),
            pl.BlockSpec((key_rows, width), lambda i, lanes: (0, lanes[i])),
            pl.BlockSpec((width, key_rows), lambda i, lanes: (lanes[i], 0)),
            pl.BlockSpec((key_rows, queries), lambda i, lanes: (0, 0)),
        ],
        out_specs=pl.BlockSpec((1, width + 16, queries), lambda i, lanes: (i, 0, 0)),
    )
    return pl.pallas_call(
        attend_kernel,
        grid_spec=grid_spec,
        out_shape=jax.ShapeDtypeStruct((count, width + 16, queries), jnp.bfloat16),
        compiler_params=pltpu.CompilerParams(vmem_limit_bytes=VMEM_BYTES),
        cost_estimate=pl.CostEstimate(
            flops=4 * count * queries * width * key_rows,
            bytes_accessed=4 * count * width * key_rows + 4 * key_rows * queries,
            transcendentals=count * queries * key_rows * width // HEAD_DIM,
        ),
        name="attend",
    )(lanes, q_blocks, gain_blocks, cosine, sine, keys, values_t, bias)


def merged(refs, width):
    heads = width // HEAD_DIM
    tails = [ref[width : width + 16, :].astype(jnp.float32) for ref in refs]
    mixed, tops, totals = [], [], []
    for head in range(heads):
        top = functools.reduce(jnp.maximum, [tail[head : head + 1] for tail in tails])
        factors = [jnp.exp2(tail[head : head + 1] - top) for tail in tails]
        cols = slice(head * HEAD_DIM, (head + 1) * HEAD_DIM)
        mixed.append(sum(ref[cols, :].astype(jnp.float32) * f for ref, f in zip(refs, factors)))
        totals.append(
            sum(tail[heads + head : heads + head + 1] * f for tail, f in zip(tails, factors))
        )
        tops.append(top)
    return mixed, tops, totals


def merge_kernel(left_ref, right_ref, out_ref):
    width = out_ref.shape[0] - 16
    mixed, tops, totals = merged([left_ref, right_ref], width)
    for head, part in enumerate(mixed):
        out_ref[head * HEAD_DIM : (head + 1) * HEAD_DIM, :] = part.astype(jnp.bfloat16)
    out_ref[width : width + 16, :] = tail_rows(tops + totals, out_ref.shape[1])


def merge_partials(left, right):
    return pl.pallas_call(
        merge_kernel,
        out_shape=jax.ShapeDtypeStruct(left.shape, jnp.bfloat16),
        cost_estimate=pl.CostEstimate(
            flops=3 * left.size, bytes_accessed=6 * left.size, transcendentals=0
        ),
        name="merge_partials",
    )(left, right)


def finish_kernel(*refs):
    out_ref = refs[-1]
    mixed, _, totals = merged(refs[:-1], out_ref.shape[1])
    for head, part in enumerate(mixed):
        cols = slice(head * HEAD_DIM, (head + 1) * HEAD_DIM)
        out_ref[:, cols] = (part / totals[head]).T.astype(jnp.bfloat16)


def finish(partials):
    rows, queries = partials[0].shape
    return pl.pallas_call(
        finish_kernel,
        out_shape=jax.ShapeDtypeStruct((queries, rows - 16), jnp.bfloat16),
        cost_estimate=pl.CostEstimate(
            flops=6 * rows * queries, bytes_accessed=10 * rows * queries, transcendentals=0
        ),
        name="finish",
    )(*partials)


def rotation_tables(position):
    angles = (
        position.astype(jnp.float32)[:, None]
        * frequencies(jnp.arange(HEAD_DIM // 2, dtype=jnp.int32).astype(jnp.float32))[None, :]
    )
    cosine, sine = jnp.cos(angles), jnp.sin(angles)
    return (
        jnp.concatenate([cosine, cosine], axis=1),
        jnp.concatenate([-sine, sine], axis=1),
    )


def line_meta(rows, order_row, length_row):
    slot = rows // CH
    ordinal = jnp.sum(
        jnp.where(slot[:, None] == jnp.arange(NCH, dtype=jnp.int32)[None, :], order_row[None, :], 0),
        axis=1,
    )
    ends = jnp.cumsum(length_row)
    request = jnp.sum((ordinal[:, None] >= ends[None, :]).astype(jnp.int32), axis=1)
    pick = request[:, None] == jnp.arange(REQS, dtype=jnp.int32)[None, :]
    start = jnp.sum(jnp.where(pick, (ends - length_row)[None, :], 0), axis=1)
    return ordinal * CH + rows % CH, start * CH


def ring_shards(
    hidden_sel,
    picked,
    order,
    lengths,
    offsets,
    cache_keys,
    cache_values,
    w_qkv,
    w_out,
    w_gate_up,
    w_down,
    gains,
):
    hidden = hidden_sel[0]
    picked_row, order_row, length_row, offset_row = picked[0], order[0], lengths[0], offsets[0]
    count = lax.axis_size("tensor")
    lane = lax.axis_index("tensor")
    group = lax.axis_index("dp")
    place = jnp.where(lane % 2 == 0, lane // 2, count - (lane + 1) // 2)
    lanes = jnp.stack([lane_at(place - r, count) for r in range(count)]).astype(jnp.int32)
    sel_dev, model_width = hidden.shape
    sel_all = sel_dev * count
    ctx_dev = cache_keys.shape[1]
    width = w_qkv.shape[2]

    hidden_swapped = swap_features(hidden, group)
    qkv_shards = dp_shards(w_qkv)
    hidden_blocks = ring_gather(hidden_swapped, count)
    qkv_full = jnp.concatenate(qkv_shards, axis=1)

    gains_swapped = swap_features(gains[2:], group)
    gain_rel = jnp.stack(
        [lax.dynamic_slice_in_dim(gains[0], lanes[r] * width, width) for r in range(count)]
    )[:, None, :]
    key_gain = lax.dynamic_slice_in_dim(gains[1], lane * width, width)
    _, query_position, _ = token_meta(picked_row, order_row, length_row, offset_row)
    cos_table, sin_table = rotation_tables(query_position)
    query_line, query_start = line_meta(picked_row, order_row, length_row)
    cache_rows = lane * ctx_dev + jnp.arange(ctx_dev, dtype=jnp.int32)
    cache_line, _ = line_meta(cache_rows, order_row, length_row)
    chosen = jnp.any(picked_row[None, :] == cache_rows[:, None], axis=1)
    cache_line = jnp.where(chosen, -1, cache_line)

    def bias_of(key_line):
        allowed = (key_line[:, None] >= query_start[None, :]) & (
            key_line[:, None] <= query_line[None, :]
        )
        return jnp.where(allowed, 0.0, NEGATIVE)

    bias_cache, bias_fresh = bias_of(cache_line), bias_of(query_line)
    piece = math.gcd(ctx_dev, CH)
    piece_rows = lane * ctx_dev + piece * jnp.arange(ctx_dev // piece, dtype=jnp.int32)
    _, piece_position, piece_local = token_meta(piece_rows, order_row, length_row, offset_row)
    turned = turn_keys(cache_keys[0], *rotation_tables(piece_position - piece_local))
    values_t = cache_values[0].T

    hidden_all = jnp.zeros((count, sel_dev, model_width), jnp.bfloat16)
    for r in range(count):
        hidden_all = lax.dynamic_update_index_in_dim(hidden_all, hidden_blocks[r], lanes[r], 0)
    hidden_all = hidden_all.reshape(sel_all, model_width)
    q_own = jnp.dot(hidden_all, qkv_full[0], preferred_element_type=jnp.float32)
    k_own = jnp.dot(hidden_all, qkv_full[1], preferred_element_type=jnp.float32)
    v_own_t = lax.dot_general(
        qkv_full[2], hidden_all, (((0,), (1,)), ((), ())), preferred_element_type=jnp.float32
    ).astype(jnp.bfloat16)
    q_sent = q_own.astype(jnp.bfloat16)
    sums = jnp.stack([jnp.sum(q_own * q_own, axis=1), jnp.sum(k_own * k_own, axis=1)])
    sums = lax.all_to_all(
        jnp.broadcast_to(sums[None], (count, 2, sel_all)),
        "tensor",
        split_axis=0,
        concat_axis=0,
        tiled=True,
    )
    q_blocks = ring_gather(q_sent, count)
    scale = lax.rsqrt(jnp.sum(sums, axis=0) / model_width + EPSILON)
    q_scale = scale[0][:, None] * (HEAD_DIM ** (-0.5) * math.log2(math.e))
    cos_q, sin_q = cos_table * q_scale, sin_table * q_scale
    k_normed = (k_own * scale[1][:, None] * key_gain[None, :]).reshape(sel_all, -1, HEAD_DIM)
    k_half = jnp.roll(k_normed, HEAD_DIM // 2, axis=2)
    k_fresh = (
        (k_normed * cos_table[:, None, :] + k_half * sin_table[:, None, :])
        .reshape(sel_all, width)
        .astype(jnp.bfloat16)
    )

    fresh = attend(
        q_sent[None],
        jnp.zeros((1,), jnp.int32),
        gain_rel[:1],
        cos_q,
        sin_q,
        k_fresh,
        v_own_t,
        bias_fresh,
    )[0]
    partials = [None] * count
    for step in range(count // 2 + 1):
        members = sorted({step, (count - step) % count})
        out = attend(
            jnp.stack([q_blocks[r] for r in members]),
            jnp.stack([lanes[r] for r in members]),
            jnp.stack([gain_rel[r] for r in members]),
            cos_q,
            sin_q,
            turned,
            values_t,
            bias_cache,
        )
        for index, r in enumerate(members):
            partials[r] = out[index]
    back, forth = ring_scatter(partials, count, merge_partials)
    attn = finish([partials[0], back, forth, fresh])

    out_shards = dp_shards(w_out)
    y_part = jnp.concatenate(
        [jnp.dot(attn, w, preferred_element_type=jnp.float32).astype(jnp.bfloat16) for w in out_shards],
        axis=1,
    )
    y_pieces = [
        lax.dynamic_slice_in_dim(y_part, lanes[r] * sel_dev, sel_dev) for r in range(count)
    ]
    back, forth = ring_scatter(y_pieces, count, add_rounded)
    y = y_pieces[0].astype(jnp.float32) + back.astype(jnp.float32) + forth.astype(jnp.float32)
    hidden_next = (hidden_swapped.astype(jnp.float32) + rms_scale(y, gains_swapped[0])).astype(
        jnp.bfloat16
    )

    gate_full = jnp.concatenate(dp_shards(w_gate_up), axis=1)
    down_full = jnp.concatenate(dp_shards(w_down), axis=1)
    rows = jnp.concatenate(ring_gather(hidden_next, count), axis=0)
    gate_part = jnp.dot(rows, gate_full[0], preferred_element_type=jnp.float32)
    up_part = jnp.dot(rows, gate_full[1], preferred_element_type=jnp.float32)
    activated = (jax.nn.silu(gate_part) * up_part).astype(jnp.bfloat16)
    z_part = jnp.dot(activated, down_full, preferred_element_type=jnp.float32).astype(jnp.bfloat16)
    z_pieces = [z_part[r * sel_dev : (r + 1) * sel_dev] for r in range(count)]
    back, forth = ring_scatter(z_pieces, count, add_rounded)
    z = z_pieces[0].astype(jnp.float32) + back.astype(jnp.float32) + forth.astype(jnp.float32)
    result = (hidden_next.astype(jnp.float32) + rms_scale(z, gains_swapped[1])).astype(jnp.bfloat16)
    result = swap_features(result, group)
    fresh_out = lax.all_to_all(k_fresh, "tensor", split_axis=0, concat_axis=1, tiled=True)
    return (result[None], fresh_out[None])


def solution(mesh):
    placed = (
        P("dp", "tensor", None),
        P("dp", None),
        P("dp", None),
        P("dp", None),
        P("dp", None),
        P("dp", "tensor", None),
        P("dp", "tensor", None),
        P(None, "dp", "tensor"),
        P("tensor", "dp"),
        P(None, "dp", "tensor"),
        P("tensor", "dp"),
        P(),
    )
    tensor, group = mesh.shape["tensor"], mesh.shape["dp"]

    def body(*arrays):
        columns = arrays[7].shape[2]
        whole_heads = columns % HEAD_DIM == 0 and tensor % 2 == 0 and group == 4
        return (ring_shards if whole_heads else shards)(*arrays)

    return jax.shard_map(
        body,
        mesh=mesh,
        in_specs=placed,
        out_specs=(P("dp", "tensor", None), P("dp", "tensor", None)),
        check_vma=False,
    )
```

```python
import functools
import math

import jax
import jax.numpy as jnp
from jax import lax
from jax.experimental import pallas as pl
from jax.experimental.pallas import tpu as pltpu
from jax.sharding import PartitionSpec as P

HEAD_DIM = 128
CH = 1024
NCH = 12
REQS = 3


THETA = 500000.0
EPSILON = 1e-06
NEGATIVE = -1e30
FLOOR = -1e28
MIB = 1024 * 1024


def token_meta(rows, order_row, length_row, offset_row):
    slot_index = rows // CH
    in_span = rows % CH
    ordinal = jnp.sum(
        jnp.where(
            slot_index[:, None] == jnp.arange(NCH, dtype=jnp.int32)[None, :], order_row[None, :], 0
        ),
        axis=1,
    )
    request_end = jnp.cumsum(length_row)
    request = jnp.sum((ordinal[:, None] >= request_end[None, :]).astype(jnp.int32), axis=1)
    request_pick = request[:, None] == jnp.arange(REQS, dtype=jnp.int32)[None, :]
    request_start = jnp.sum(jnp.where(request_pick, (request_end - length_row)[None, :], 0), axis=1)
    request_shift = jnp.sum(jnp.where(request_pick, offset_row[None, :], 0), axis=1)
    position = request_shift + (ordinal - request_start) * CH + in_span
    return (request, position, in_span)


def frequencies(index_float):
    return jnp.exp(index_float * (-2.0 * math.log(THETA) / HEAD_DIM))


def rope_full(values_in, position):
    row_count = values_in.shape[0]
    half_dim = HEAD_DIM // 2
    split = values_in.reshape(row_count, -1, HEAD_DIM)
    angles = (
        position.astype(jnp.float32)[:, None]
        * frequencies(jnp.arange(half_dim, dtype=jnp.int32).astype(jnp.float32))[None, :]
    )
    cosine = jnp.cos(angles)[:, None, :]
    sine = jnp.sin(angles)[:, None, :]
    first = split[..., :half_dim]
    second = split[..., half_dim:]
    turned = jnp.concatenate(
        [first * cosine - second * sine, second * cosine + first * sine], axis=-1
    )
    return turned.reshape(row_count, -1)


def rms_scale(values_in, gain):
    return (
        values_in
        * lax.rsqrt(jnp.mean(values_in * values_in, axis=-1, keepdims=True) + EPSILON)
        * gain
    )


def shards(
    hidden_sel,
    picked,
    order,
    lengths,
    offsets,
    cache_keys,
    cache_values,
    w_qkv,
    w_out,
    w_gate_up,
    w_down,
    gains,
):
    hidden = hidden_sel[0]
    picked_row = picked[0]
    order_row = order[0]
    length_row = lengths[0]
    offset_row = offsets[0]
    keys_local = cache_keys[0]
    values_local = cache_values[0]
    lane_count = lax.axis_size("tensor")
    lane_index = lax.axis_index("tensor")
    sel_dev = hidden.shape[0]
    sel_all = sel_dev * lane_count
    ctx_dev = keys_local.shape[0]
    model_width = hidden.shape[1]
    head_count = model_width // HEAD_DIM
    qkv_full, out_full = (
        lax.all_gather(w_qkv, "dp", axis=1, tiled=True),
        lax.all_gather(w_out, "dp", axis=1, tiled=True),
    )
    query_request, query_position, _ = token_meta(picked_row, order_row, length_row, offset_row)
    cache_rows = lane_index * ctx_dev + jnp.arange(ctx_dev, dtype=jnp.int32)
    cache_request, cache_position, cache_local = token_meta(
        cache_rows, order_row, length_row, offset_row
    )
    chosen = jnp.any(picked_row[:, None] == cache_rows[None, :], axis=0)
    fresh_request = lax.dynamic_slice_in_dim(query_request, lane_index * sel_dev, sel_dev)
    fresh_position = lax.dynamic_slice_in_dim(query_position, lane_index * sel_dev, sel_dev)
    projected = jnp.einsum(
        "nd,kdc->knc",
        lax.all_gather(hidden, "tensor", axis=0, tiled=True),
        qkv_full,
        preferred_element_type=jnp.float32,
    )
    own_rows = lax.all_to_all(
        projected.astype(jnp.bfloat16), "tensor", split_axis=1, concat_axis=2, tiled=True
    ).astype(projected.dtype)
    query_tok = rope_full(rms_scale(own_rows[0], gains[0]), fresh_position).astype(jnp.bfloat16)
    key_fresh = rope_full(rms_scale(own_rows[1], gains[1]), fresh_position).astype(jnp.bfloat16)
    value_fresh = own_rows[2].astype(jnp.bfloat16)
    queries = lax.all_gather(query_tok, "tensor", axis=0, tiled=True)
    turned_keys = rope_full(keys_local.astype(jnp.float32), cache_position - cache_local).astype(
        jnp.bfloat16
    )
    all_keys = jnp.concatenate([turned_keys, key_fresh], axis=0).reshape(-1, head_count, HEAD_DIM)
    all_values = jnp.concatenate([values_local, value_fresh], axis=0).reshape(
        -1, head_count, HEAD_DIM
    )
    key_request = jnp.concatenate([cache_request, fresh_request])
    key_position = jnp.concatenate([cache_position, fresh_position])
    key_live = jnp.concatenate([jnp.logical_not(chosen), jnp.ones((sel_dev,), bool)])
    block_rows = min(512, sel_all)
    block_count = sel_all // block_rows

    def attend(operands):
        query_block, block_request, block_position = operands
        scores = jnp.einsum(
            "qhd,khd->hqk",
            query_block.reshape(block_rows, head_count, HEAD_DIM),
            all_keys,
            preferred_element_type=jnp.float32,
        ) * HEAD_DIM ** (-0.5)
        usable = (
            (block_request[:, None] == key_request[None, :])
            & (key_position[None, :] <= block_position[:, None])
            & key_live[None, :]
        )
        masked = jnp.where(usable[None], scores, NEGATIVE)
        local_max = jnp.max(masked, axis=2)
        weights = jnp.where(usable[None], jnp.exp(masked - local_max[:, :, None]), 0.0)
        totals = jnp.sum(weights, axis=2)
        mixed = jnp.einsum(
            "hqk,khd->qhd",
            weights.astype(jnp.bfloat16),
            all_values,
            preferred_element_type=jnp.float32,
        )
        return (mixed.reshape(block_rows, model_width), local_max.T, totals.T)

    partial_out, local_max, totals = lax.map(
        attend,
        (
            queries.reshape(block_count, block_rows, model_width),
            query_request.reshape(block_count, block_rows),
            query_position.reshape(block_count, block_rows),
        ),
    )
    partial_out = partial_out.reshape(sel_all, model_width)
    local_max = local_max.reshape(sel_all, head_count)
    totals = totals.reshape(sel_all, head_count)
    row_max = lax.pmax(local_max.astype(jnp.bfloat16), "tensor").astype(local_max.dtype)
    factor = jnp.exp(local_max - row_max)
    scaled_out = (partial_out.reshape(sel_all, head_count, HEAD_DIM) * factor[:, :, None]).reshape(
        sel_all, model_width
    )
    scaled_total = totals * factor
    summed = lax.psum_scatter(
        scaled_out.astype(jnp.bfloat16), "tensor", scatter_dimension=0, tiled=True
    ).astype(jnp.float32)
    weight_sum = lax.psum_scatter(
        scaled_total.astype(jnp.bfloat16), "tensor", scatter_dimension=0, tiled=True
    ).astype(jnp.float32)
    attn_rows = (
        (summed.reshape(sel_dev, head_count, HEAD_DIM) / weight_sum[:, :, None])
        .reshape(sel_dev, model_width)
        .astype(jnp.bfloat16)
    )
    attn_cols = lax.all_to_all(attn_rows, "tensor", split_axis=1, concat_axis=0, tiled=True)
    attn_proj = lax.psum_scatter(
        jnp.dot(attn_cols, out_full, preferred_element_type=jnp.float32).astype(jnp.bfloat16),
        "tensor",
        scatter_dimension=0,
        tiled=True,
    ).astype(jnp.float32)
    hidden_next = (hidden.astype(jnp.float32) + rms_scale(attn_proj, gains[2])).astype(jnp.bfloat16)
    gate_full, down_full = (
        lax.all_gather(w_gate_up, "dp", axis=1, tiled=True),
        lax.all_gather(w_down, "dp", axis=1, tiled=True),
    )
    rows_piece = lax.all_gather(hidden_next, "tensor", axis=0, tiled=True)
    gate_part = jnp.dot(rows_piece, gate_full[0], preferred_element_type=jnp.float32)
    up_part = jnp.dot(rows_piece, gate_full[1], preferred_element_type=jnp.float32)
    activated = (jax.nn.silu(gate_part) * up_part).astype(jnp.bfloat16)
    mlp_out = lax.psum_scatter(
        jnp.dot(activated, down_full, preferred_element_type=jnp.float32).astype(jnp.bfloat16),
        "tensor",
        scatter_dimension=0,
        tiled=True,
    ).astype(jnp.float32)
    result = (hidden_next.astype(jnp.float32) + rms_scale(mlp_out, gains[3])).astype(jnp.bfloat16)
    return (result[None], key_fresh[None])


def lane_at(place, count):
    place = (place + count) % count
    return jnp.where(place < count // 2, 2 * place, 2 * (count - place) - 1)


def lane_back(distance, count):
    lane = lax.axis_index("tensor")
    place = jnp.where(lane % 2 == 0, lane // 2, count - (lane + 1) // 2)
    return lane_at(place - distance, count)


def ring_steps(count, shift):
    around = list(range(0, count, 2)) + list(range(count - 1, 0, -2))
    return [(around[i], around[(i + shift) % count]) for i in range(count)]


def ring_gather(block, count, work=None):
    blocks = [block] + [None] * (count - 1)
    forth = back = block
    work = work or (lambda step, blocks: None)
    made = None
    for step in range(1, count // 2 + 1):
        if made is not None:
            (forth, back), kept = lax.optimization_barrier(((forth, back), made.value))
            made.value = kept
        forth = lax.ppermute(forth, "tensor", ring_steps(count, 1))
        blocks[step] = forth
        if step < count - step:
            back = lax.ppermute(back, "tensor", ring_steps(count, -1))
            blocks[count - step] = back
            if step == 1:
                forth, back = lax.optimization_barrier((forth, back))
        made = work(step - 1, blocks)
    work(count // 2, blocks)
    return blocks


class Made:
    def __init__(self, value):
        self.value = value


def ring_scatter(pieces, count, merge, more=None):
    half = count // 2
    back, forth = pieces[half], pieces[half + 1]
    arrived = None
    for step in range(1, half + 1):
        back = lax.ppermute(back, "tensor", ring_steps(count, -1))
        if step < half:
            forth = lax.ppermute(forth, "tensor", ring_steps(count, 1))
        if more is not None:
            more(step, arrived)
        arrived = back
        if step < half:
            back = merge(back, pieces[half - step])
        if step < half - 1:
            forth = merge(forth, pieces[half + 1 + step])
    return back, forth


def add_rounded(left, right):
    return (left.astype(jnp.float32) + right.astype(jnp.float32)).astype(jnp.bfloat16)


def dp_whole(weight, axis=1):
    return lax.all_gather(weight, "dp", axis=axis, tiled=True)


def upright(row):
    wide = jnp.broadcast_to(row.astype(jnp.float32), (HEAD_DIM, row.shape[1]))
    return wide.T


def prepare_kernel(
    order_ref, lengths_ref, offsets_ref, picked_ref, bias_ref, fresh_ref, angles_ref, piece_ref
):
    lane = lax.axis_index("tensor")
    ends = [lengths_ref[0, 0]]
    for request in range(1, REQS):
        ends.append(ends[-1] + lengths_ref[0, request])
    starts = [ends[request] - lengths_ref[0, request] for request in range(REQS)]

    def placed(ordinal):
        start = jnp.where(ordinal >= ends[0], starts[1], starts[0])
        shift = jnp.where(ordinal >= ends[0], offsets_ref[0, 1], offsets_ref[0, 0])
        for request in range(2, REQS):
            start = jnp.where(ordinal >= ends[request - 1], starts[request], start)
            shift = jnp.where(ordinal >= ends[request - 1], offsets_ref[0, request], shift)
        return start, shift

    picked = picked_ref[...]
    slot, local = picked // CH, picked % CH
    ordinal = jnp.zeros_like(picked)
    for index in range(NCH):
        ordinal = jnp.where(slot == index, order_ref[0, index], ordinal)
    start, shift = placed(ordinal)
    line, line_start = ordinal * CH + local, start * CH
    position = shift + (ordinal - start) * CH + local

    at = lax.broadcasted_iota(jnp.int32, (1, HEAD_DIM), 1) % (HEAD_DIM // 2)
    speed = frequencies(at.astype(jnp.float32))
    angles_ref[...] = upright(position) * speed
    line_column = upright(line)[:, :1].astype(jnp.int32)

    def bias_of(key_line):
        allowed = (key_line >= line_start) & (key_line <= line)
        return jnp.where(allowed, 0.0, NEGATIVE)

    fresh_ref[...] = bias_of(line_column).astype(jnp.bfloat16)
    rows = bias_ref.shape[0]
    piece = math.gcd(rows, CH)
    shifts = jnp.zeros((8, HEAD_DIM), jnp.float32)
    piece_at = lax.broadcasted_iota(jnp.int32, (8, HEAD_DIM), 0)
    for index in range(rows // piece):
        first = lane * rows + index * piece
        piece_slot = first // CH
        piece_ordinal = order_ref[0, piece_slot]
        piece_start, piece_shift = placed(piece_ordinal)
        moved = (piece_shift + (piece_ordinal - piece_start) * CH).astype(jnp.float32)
        shifts = jnp.where(piece_at == index, moved, shifts)
        row = first + lax.broadcasted_iota(jnp.int32, (piece, 1), 0)
        chosen = jnp.max(jnp.where(row == picked, 1.0, 0.0), axis=1, keepdims=True) > 0.5
        key_line = jnp.where(chosen, -1, piece_ordinal * CH + row % CH)
        bias_ref[index * piece : (index + 1) * piece, :] = bias_of(key_line).astype(jnp.bfloat16)
    piece_ref[...] = shifts * speed


def prepare(order, lengths, offsets, picked, ctx_dev):
    queries = picked.shape[1]
    smem = pl.BlockSpec(memory_space=pltpu.SMEM)
    vmem = pl.BlockSpec(memory_space=pltpu.VMEM)
    return pl.pallas_call(
        prepare_kernel,
        in_specs=[smem, smem, smem, vmem],
        out_specs=[vmem] * 4,
        out_shape=[
            jax.ShapeDtypeStruct((ctx_dev, queries), jnp.bfloat16),
            jax.ShapeDtypeStruct((queries, queries), jnp.bfloat16),
            jax.ShapeDtypeStruct((queries, HEAD_DIM), jnp.float32),
            jax.ShapeDtypeStruct((8, HEAD_DIM), jnp.float32),
        ],
        compiler_params=pltpu.CompilerParams(vmem_limit_bytes=57 * MIB),
        cost_estimate=pl.CostEstimate(
            flops=8 * ctx_dev * queries, bytes_accessed=4 * ctx_dev * queries, transcendentals=0
        ),
        name="prepare",
    )(order, lengths, offsets, picked)


def turn_kernel(first, piece, cos_ref, sin_ref, keys_ref, out_ref, buffer, sems):
    parts, rows, width = buffer.shape
    loads, stores = [], []
    for part in range(parts):
        loads.append(
            pltpu.make_async_copy(
                keys_ref.at[pl.ds(first + part * rows, rows), :], buffer.at[part], sems.at[0, part]
            )
        )
        stores.append(
            pltpu.make_async_copy(
                buffer.at[part], out_ref.at[pl.ds(part * rows, rows), :], sems.at[1, part]
            )
        )
        loads[part].start()
    for part in range(parts):
        at = (first + part * rows) // piece
        cosine, sine = cos_ref[at : at + 1, :], sin_ref[at : at + 1, :]
        loads[part].wait()
        for head in range(width // HEAD_DIM):
            cols = slice(head * HEAD_DIM, (head + 1) * HEAD_DIM)
            held = buffer[part, :, cols].astype(jnp.float32)
            turned = held * cosine + pltpu.roll(held, HEAD_DIM // 2, 1) * sine
            buffer[part, :, cols] = turned.astype(jnp.bfloat16)
        stores[part].start()
    for part in range(parts):
        stores[part].wait()


def turn_keys(first, rows, piece, keys, cosine, sine):
    width = keys.shape[1]
    per = math.gcd(math.gcd(rows, piece), 128)
    vmem = pl.BlockSpec(memory_space=pltpu.VMEM)
    whole = pl.BlockSpec(memory_space=pltpu.HBM)
    return pl.pallas_call(
        functools.partial(turn_kernel, first, piece),
        in_specs=[vmem, vmem, whole],
        out_specs=whole,
        out_shape=jax.ShapeDtypeStruct((rows, width), jnp.bfloat16),
        scratch_shapes=[
            pltpu.VMEM((rows // per, per, width), jnp.bfloat16),
            pltpu.SemaphoreType.DMA((2, rows // per)),
        ],
        compiler_params=pltpu.CompilerParams(vmem_limit_bytes=57 * MIB),
        cost_estimate=pl.CostEstimate(
            flops=4 * rows * width, bytes_accessed=4 * rows * width, transcendentals=0
        ),
        name="turn_keys",
    )(cosine, sine, keys)


def project_kernel(distances, earlier, *refs):
    blocks = len(distances)
    hidden_refs, refs = refs[:blocks], refs[blocks:]
    (weight_ref, gain_ref, cos_ref, sin_ref), refs = refs[:4], refs[4:]
    before, refs = refs[: 4 * len(earlier)], refs[4 * len(earlier) :]
    last = bool(earlier)
    (q_ref, k_ref, v_ref), refs = refs[:3], refs[3:]
    all_sums, rows_ref = (refs[1], refs[0]) if last else refs
    sel_dev = hidden_refs[0].shape[0]
    count = cos_ref.shape[0] // sel_dev
    width = weight_ref.shape[2]
    lane = lax.axis_index("tensor")

    def token_rows(distance):
        at = lane_back(distance, count) * sel_dev
        return pl.ds(pl.multiple_of(at, sel_dev), sel_dev)

    for index in range(blocks):
        rows_ref[index * sel_dev : (index + 1) * sel_dev, :] = hidden_refs[index][...]

    def project(kind):
        return jnp.dot(rows_ref[...], weight_ref[kind], preferred_element_type=jnp.float32)

    own = pl.ds(pl.multiple_of(lane * width, width), width)
    turned, squares = [], []
    tables = [
        jnp.concatenate([table[token_rows(d), :] for d in distances], axis=0)
        for table in (cos_ref, sin_ref)
    ]
    for kind in (0, 1):
        raw = project(kind)
        squares.append(jnp.sum(raw * raw, axis=1, keepdims=True))
        raw = raw * gain_ref[kind : kind + 1, own]
        turned.append([])
        for head in range(width // HEAD_DIM):
            part = raw[:, head * HEAD_DIM : (head + 1) * HEAD_DIM]
            turned[kind].append(part * tables[0] + pltpu.roll(part, HEAD_DIM // 2, 1) * tables[1])
    values = project(2)
    at = lax.broadcasted_iota(jnp.int32, (blocks * sel_dev, HEAD_DIM), 1)
    sums = jnp.where(at < HEAD_DIM // 2, squares[0], squares[1])
    for index, distance in enumerate(distances):
        rows = slice(index * sel_dev, (index + 1) * sel_dev)
        to = token_rows(distance) if last else rows
        for head in range(width // HEAD_DIM):
            cols = slice(head * HEAD_DIM, (head + 1) * HEAD_DIM)
            q_ref[to, cols] = turned[0][head][rows].astype(jnp.bfloat16)
            k_ref[to, cols] = turned[1][head][rows]
        v_ref[to, :] = values[rows].astype(jnp.bfloat16)
        all_sums[to, :] = sums[rows]
    for call, members in enumerate(earlier):
        for index, distance in enumerate(members):
            rows = slice(index * sel_dev, (index + 1) * sel_dev)
            to = token_rows(distance)
            for source, target in zip(before[4 * call : 4 * call + 4], (q_ref, k_ref, v_ref, all_sums)):
                target[to, :] = source[rows, :]
    if last:
        across = all_sums[...].T
        row = lax.broadcasted_iota(jnp.int32, (16, width), 0)
        tail = jnp.zeros((16, width), jnp.float32)
        at = 0
        for kind in (0, 1):
            line = across[kind * (HEAD_DIM // 2) : kind * (HEAD_DIM // 2) + 1]
            upper = line.astype(jnp.bfloat16).astype(jnp.float32)
            for part in (upper, line - upper):
                for start in range(0, line.shape[1], width):
                    tail = jnp.where(row == at, part[:, start : start + width], tail)
                    at += 1
        q_ref[line.shape[1] :, :] = tail.astype(jnp.bfloat16)


def project(distances, blocks, weight, gains, cosine, sine, earlier=(), outputs=()):
    sel_dev, model_width = blocks[0].shape
    width = weight.shape[2]
    last = bool(earlier)
    queries = cosine.shape[0] if last else sel_dev * len(blocks)
    vmem = pl.BlockSpec(memory_space=pltpu.VMEM)
    out_shape = [
        jax.ShapeDtypeStruct((queries + (16 if last else 0), width), jnp.bfloat16),
        jax.ShapeDtypeStruct((queries, width), jnp.float32),
        jax.ShapeDtypeStruct((queries, width), jnp.bfloat16),
    ]
    scratch = [pltpu.VMEM((sel_dev * len(blocks), model_width), jnp.bfloat16)]
    if last:
        scratch.append(pltpu.VMEM((queries, HEAD_DIM), jnp.float32))
    else:
        out_shape.append(jax.ShapeDtypeStruct((queries, HEAD_DIM), jnp.float32))
    return pl.pallas_call(
        functools.partial(project_kernel, distances, earlier),
        in_specs=[vmem] * (len(blocks) + 4 + len(outputs)),
        out_specs=[vmem] * len(out_shape),
        out_shape=out_shape,
        scratch_shapes=scratch,
        compiler_params=pltpu.CompilerParams(vmem_limit_bytes=16 * MIB),
        cost_estimate=pl.CostEstimate(
            flops=6 * sel_dev * len(blocks) * width * model_width,
            bytes_accessed=6 * model_width * width,
            transcendentals=0,
        ),
        name="project",
    )(*blocks, weight, gains, cosine, sine, *outputs)


def scales_kernel(model_width, *refs):
    out_ref = refs[-1]
    queries = out_ref.shape[1]
    width = refs[0].shape[1]
    tail = sum(ref[queries:, :].astype(jnp.float32) for ref in refs[:-1])
    rows = queries // width
    for kind in (0, 1):
        for index in range(rows):
            upper = tail[2 * rows * kind + index : 2 * rows * kind + index + 1]
            lower = tail[2 * rows * kind + rows + index : 2 * rows * kind + rows + index + 1]
            scale = lax.rsqrt((upper + lower) / model_width + EPSILON)
            if kind == 0:
                scale = scale * (HEAD_DIM ** (-0.5) * math.log2(math.e))
            out_ref[kind : kind + 1, index * width : (index + 1) * width] = scale


def scales(blocks, model_width):
    rows, width = blocks[0].shape
    vmem = pl.BlockSpec(memory_space=pltpu.VMEM)
    return pl.pallas_call(
        functools.partial(scales_kernel, model_width),
        in_specs=[vmem] * len(blocks),
        out_specs=vmem,
        out_shape=jax.ShapeDtypeStruct((2, rows - 16), jnp.float32),
        compiler_params=pltpu.CompilerParams(vmem_limit_bytes=8 * MIB),
        cost_estimate=pl.CostEstimate(flops=rows, bytes_accessed=rows, transcendentals=rows),
        name="scales",
    )(*blocks)


def tail_rows(rows, wide):
    at = lax.broadcasted_iota(jnp.int32, (16, wide), 0)
    tail = jnp.zeros((16, wide), jnp.float32)
    for index, row in enumerate(rows):
        tail = jnp.where(at == index, row, tail)
    return tail.astype(jnp.bfloat16)


def attend_one(q_ref, key_refs, value_ref, columns, scale_ref, bias_ref, out_ref):
    width = q_ref.shape[1]
    queries = scale_ref.shape[1]
    scale = scale_ref[0:1, :]
    parts, start = [], 0
    for ref in key_refs:
        parts.append(slice(start, start + ref.shape[0]))
        start += ref.shape[0]
    raw = [
        [
            lax.dot_general(
                ref[:, cols],
                q_ref[:queries, head * HEAD_DIM : (head + 1) * HEAD_DIM],
                (((1,), (1,)), ((), ())),
                preferred_element_type=jnp.float32,
            )
            for ref in key_refs
        ]
        for head, cols in enumerate(columns)
    ]
    tops, totals = [], []
    for head, cols in enumerate(columns):
        scores = [
            part * scale + bias_ref[rows, :].astype(jnp.float32)
            for part, rows in zip(raw[head], parts)
        ]
        top = functools.reduce(
            jnp.maximum, [jnp.max(part, axis=0, keepdims=True) for part in scores]
        )
        top = jnp.maximum(top, FLOOR).astype(jnp.bfloat16).astype(jnp.float32)
        weights = [jnp.exp2(part - top) for part in scores]
        tops.append(top)
        totals.append(sum(jnp.sum(part, axis=0, keepdims=True) for part in weights))
        mixed = sum(
            lax.dot_general(
                value_ref[rows, cols],
                part.astype(jnp.bfloat16),
                (((0,), (0,)), ((), ())),
                preferred_element_type=jnp.float32,
            )
            for rows, part in zip(parts, weights)
        )
        out_ref[head * HEAD_DIM : (head + 1) * HEAD_DIM, :] = mixed.astype(jnp.bfloat16)
    out_ref[width : width + 16, :] = tail_rows(tops + totals, queries)


def fresh_kernel(scale_ref, bias_ref, q_ref, k_ref, v_ref, out_ref, keys_ref):
    columns = [
        slice(start, start + HEAD_DIM) for start in range(0, q_ref.shape[1], HEAD_DIM)
    ]
    scale = upright(scale_ref[1:2, :])
    for cols in columns:
        keys_ref[:, cols] = (k_ref[:, cols] * scale).astype(jnp.bfloat16)
    attend_one(q_ref, [keys_ref], v_ref, columns, scale_ref, bias_ref, out_ref)


def attend_kernel(distances, devices, scale_ref, bias_ref, *refs):
    count = len(distances)
    q_refs, kv_refs, out_refs = refs[:count], refs[count:-count], refs[-count:]
    width = q_refs[0].shape[1]
    for index, distance in enumerate(distances):
        lane = lane_back(distance, devices)
        columns = [
            pl.ds(pl.multiple_of(lane * width + start, HEAD_DIM), HEAD_DIM)
            for start in range(0, width, HEAD_DIM)
        ]
        attend_one(
            q_refs[index],
            kv_refs[:-1],
            kv_refs[-1],
            columns,
            scale_ref,
            bias_ref,
            out_refs[index],
        )


def attend_cost(count, queries, width, key_rows):
    return pl.CostEstimate(
        flops=4 * count * queries * width * key_rows,
        bytes_accessed=4 * count * width * key_rows,
        transcendentals=count * queries * key_rows * width // HEAD_DIM,
    )


def attend_fresh(query, keys, values, scale, bias):
    queries, width = values.shape
    vmem = pl.BlockSpec(memory_space=pltpu.VMEM)
    return pl.pallas_call(
        fresh_kernel,
        in_specs=[vmem] * 5,
        out_specs=vmem,
        out_shape=jax.ShapeDtypeStruct((width + 16, queries), jnp.bfloat16),
        scratch_shapes=[pltpu.VMEM((queries, width), jnp.bfloat16)],
        compiler_params=pltpu.CompilerParams(vmem_limit_bytes=16 * MIB),
        cost_estimate=attend_cost(1, queries, width, queries),
        name="attend_fresh",
    )(scale, bias, query, keys, values)


def attend(distances, devices, blocks, scale, keys, values, bias):
    count = len(blocks)
    width = blocks[0].shape[1]
    key_rows, queries = bias.shape
    vmem = pl.BlockSpec(memory_space=pltpu.VMEM)
    return pl.pallas_call(
        functools.partial(attend_kernel, distances, devices),
        in_specs=[vmem] * (3 + count + len(keys)),
        out_specs=[vmem] * count,
        out_shape=[jax.ShapeDtypeStruct((width + 16, queries), jnp.bfloat16)] * count,
        compiler_params=pltpu.CompilerParams(vmem_limit_bytes=28 * MIB),
        cost_estimate=attend_cost(count, queries, width, key_rows),
        name="attend",
    )(scale, bias, *blocks, *keys, values)


def merged(refs, width):
    heads = width // HEAD_DIM
    tails = [ref[width : width + 16, :].astype(jnp.float32) for ref in refs]
    mixed, tops, totals = [], [], []
    for head in range(heads):
        top = functools.reduce(jnp.maximum, [tail[head : head + 1] for tail in tails])
        factors = [jnp.exp2(tail[head : head + 1] - top) for tail in tails]
        cols = slice(head * HEAD_DIM, (head + 1) * HEAD_DIM)
        mixed.append(sum(ref[cols, :].astype(jnp.float32) * f for ref, f in zip(refs, factors)))
        totals.append(
            sum(tail[heads + head : heads + head + 1] * f for tail, f in zip(tails, factors))
        )
        tops.append(top)
    return mixed, tops, totals


def merge_kernel(left_ref, right_ref, out_ref):
    width = out_ref.shape[0] - 16
    mixed, tops, totals = merged([left_ref, right_ref], width)
    for head, part in enumerate(mixed):
        out_ref[head * HEAD_DIM : (head + 1) * HEAD_DIM, :] = part.astype(jnp.bfloat16)
    out_ref[width : width + 16, :] = tail_rows(tops + totals, out_ref.shape[1])


def merge_partials(left, right):
    vmem = pl.BlockSpec(memory_space=pltpu.VMEM)
    return pl.pallas_call(
        merge_kernel,
        in_specs=[vmem, vmem],
        out_specs=vmem,
        out_shape=jax.ShapeDtypeStruct(left.shape, jnp.bfloat16),
        compiler_params=pltpu.CompilerParams(vmem_limit_bytes=4 * MIB),
        cost_estimate=pl.CostEstimate(
            flops=3 * left.size, bytes_accessed=6 * left.size, transcendentals=0
        ),
        name="merge_partials",
    )(left, right)


def output_kernel(*refs):
    partial_refs, weight_ref, out_refs = refs[:4], refs[4], refs[5:-2]
    attn_ref, rows_ref = refs[-2:]
    width = attn_ref.shape[1]
    count, sel_dev = len(out_refs), out_refs[0].shape[0]
    mixed, _, totals = merged(partial_refs, width)
    for head, part in enumerate(mixed):
        cols = slice(head * HEAD_DIM, (head + 1) * HEAD_DIM)
        attn_ref[:, cols] = (part / totals[head]).T.astype(jnp.bfloat16)
    rows_ref[...] = jnp.dot(
        attn_ref[...], weight_ref[...], preferred_element_type=jnp.float32
    ).astype(jnp.bfloat16)
    for r in range(count):
        at = pl.multiple_of(lane_back(r, count) * sel_dev, sel_dev)
        out_refs[r][...] = rows_ref[pl.ds(at, sel_dev), :]


def output_rows(partials, weight, count):
    queries = partials[0].shape[1]
    width, model_width = weight.shape
    vmem = pl.BlockSpec(memory_space=pltpu.VMEM)
    return pl.pallas_call(
        output_kernel,
        in_specs=[vmem] * 5,
        out_specs=[vmem] * count,
        out_shape=[jax.ShapeDtypeStruct((queries // count, model_width), jnp.bfloat16)] * count,
        scratch_shapes=[
            pltpu.VMEM((queries, width), jnp.bfloat16),
            pltpu.VMEM((queries, model_width), jnp.bfloat16),
        ],
        compiler_params=pltpu.CompilerParams(vmem_limit_bytes=16 * MIB),
        cost_estimate=pl.CostEstimate(
            flops=2 * queries * width * model_width,
            bytes_accessed=2 * width * model_width + 2 * queries * model_width,
            transcendentals=0,
        ),
        name="output_rows",
    )(*partials, weight)


def feed_kernel(*refs):
    count = (len(refs) - 3) // 2
    row_refs, (up_ref, down_ref), out_refs = refs[:count], refs[count : count + 2], refs[count + 2 : -1]
    rows_ref = refs[-1]
    sel_dev, model_width = row_refs[0].shape
    units = up_ref.shape[2]
    per = math.gcd(units, 256)
    for r in range(count):
        rows_ref[r * sel_dev : (r + 1) * sel_dev, :] = row_refs[r][...]
    active = []
    for start in range(0, units, per):
        gate, up = [
            jnp.dot(
                rows_ref[...],
                up_ref[kind, :, start : start + per],
                preferred_element_type=jnp.float32,
            )
            for kind in (0, 1)
        ]
        active.append((gate * jax.nn.sigmoid(gate) * up).astype(jnp.bfloat16))
    active = jnp.concatenate(active, axis=1)
    wide = math.gcd(model_width, 512)
    for start in range(0, model_width, wide):
        cols = slice(start, start + wide)
        part = jnp.dot(active, down_ref[:, cols], preferred_element_type=jnp.float32)
        for r in range(count):
            out_refs[r][:, cols] = part[r * sel_dev : (r + 1) * sel_dev].astype(jnp.bfloat16)


def feed_forward(row_blocks, up_weight, down_weight):
    count = len(row_blocks)
    sel_dev, model_width = row_blocks[0].shape
    units = up_weight.shape[2]
    queries = count * sel_dev
    vmem = pl.BlockSpec(memory_space=pltpu.VMEM)
    return pl.pallas_call(
        feed_kernel,
        in_specs=[vmem] * (count + 2),
        out_specs=[vmem] * count,
        out_shape=[jax.ShapeDtypeStruct((sel_dev, model_width), jnp.bfloat16)] * count,
        scratch_shapes=[pltpu.VMEM((queries, model_width), jnp.bfloat16)],
        compiler_params=pltpu.CompilerParams(vmem_limit_bytes=16 * MIB),
        cost_estimate=pl.CostEstimate(
            flops=6 * queries * model_width * units,
            bytes_accessed=4 * queries * model_width,
            transcendentals=queries * units,
        ),
        name="feed_forward",
    )(*row_blocks, up_weight, down_weight)


def rotation_tables(angles):
    flip = jnp.where(jnp.arange(HEAD_DIM) < HEAD_DIM // 2, -1.0, 1.0)
    return jnp.cos(angles), jnp.sin(angles) * flip


def ring_shards(
    hidden_sel,
    picked,
    order,
    lengths,
    offsets,
    cache_keys,
    cache_values,
    w_qkv,
    w_out,
    w_gate_up,
    w_down,
    gains,
):
    hidden = hidden_sel[0]
    count = lax.axis_size("tensor")
    sel_dev, model_width = hidden.shape
    sel_all = sel_dev * count
    ctx_dev = cache_keys.shape[1]

    half = count // 2
    near = [0, 1, count - 1]
    middle = [r for r in range(count) if r not in near and r != half]

    qkv_full = dp_whole(w_qkv)
    piece = math.gcd(ctx_dev, CH)
    bias_cache, bias_fresh, angles, piece_angles = prepare(order, lengths, offsets, picked, ctx_dev)
    cos_table, sin_table = rotation_tables(angles)
    hidden_blocks = ring_gather(hidden, count)
    w_out, w_gate_up, w_down, hidden_blocks[1] = lax.optimization_barrier(
        (w_out, w_gate_up, w_down, hidden_blocks[1])
    )
    out_full, up_full, down_full = dp_whole(w_out), dp_whole(w_gate_up), dp_whole(w_down)
    outputs, calls = [], [near, middle]
    for members in calls:
        outputs += project(
            members, [hidden_blocks[r] for r in members], qkv_full, gains, cos_table, sin_table
        )
    q_sent, k_turned, v_own = project(
        [half],
        [hidden_blocks[half]],
        qkv_full,
        gains,
        cos_table,
        sin_table,
        earlier=calls,
        outputs=outputs,
    )

    q_sent, piece_angles, k_sent = lax.optimization_barrier(
        (q_sent, piece_angles, k_turned.astype(jnp.bfloat16))
    )
    cos_piece, sin_piece = rotation_tables(piece_angles)
    turned = []

    def turn_work(step, blocks):
        if step in (0, 1):
            rows = ctx_dev // 2
            made = Made(turn_keys(step * rows, rows, piece, cache_keys[0], cos_piece, sin_piece))
            turned.append(made)
            return made
        return None

    q_blocks = ring_gather(q_sent, count, turn_work)
    turned = [made.value for made in turned]
    k_sent, q_blocks[1] = lax.optimization_barrier((k_sent, q_blocks[1]))
    fresh_out = lax.all_to_all(k_sent, "tensor", split_axis=0, concat_axis=1, tiled=True)
    fresh_out, q_blocks[half] = lax.optimization_barrier((fresh_out, q_blocks[half]))
    scale = scales(q_blocks, model_width)
    own_scale = lax.dynamic_slice_in_dim(scale[1], lax.axis_index("tensor") * sel_dev, sel_dev)
    fresh_out = (fresh_out.astype(jnp.float32) * own_scale[:, None]).astype(jnp.bfloat16)

    partials = [None] * count
    fresh = []

    def attend_members(members, arrived):
        blocks = [q_blocks[r] for r in members]
        if arrived is not None:
            blocks, _ = lax.optimization_barrier((blocks, arrived))
        out = attend(members, count, blocks, scale, turned, cache_values[0], bias_cache)
        for r, made in zip(members, out):
            partials[r] = made

    def attend_more(step, arrived):
        if step < half:
            attend_members(sorted({half - step, half + 1 + step} - {count}), arrived)
        else:
            attend_members([0], arrived)
            fresh.append(attend_fresh(q_sent, k_turned, v_own, scale, bias_fresh))

    attend_members([half, half + 1], None)
    back, forth = ring_scatter(partials, count, merge_partials, attend_more)
    fresh = fresh[0]

    y_pieces = output_rows([partials[0], back, forth, fresh], out_full, count)
    back, forth = ring_scatter(y_pieces, count, add_rounded)
    y = y_pieces[0].astype(jnp.float32) + back.astype(jnp.float32) + forth.astype(jnp.float32)
    hidden_next = (hidden.astype(jnp.float32) + rms_scale(y, gains[2])).astype(jnp.bfloat16)

    fed = []

    def feed_work(step, blocks):
        members = {1: near, half - 1: middle, half: [half]}.get(step)
        if not members:
            return None
        rows = [blocks[r] for r in members]
        if step == half:
            rows, fed[-1][1].value = lax.optimization_barrier((rows, fed[-1][1].value))
        made = Made(feed_forward(rows, up_full, down_full))
        fed.append((members, made))
        return made

    ring_gather(hidden_next, count, feed_work)
    z_pieces = [None] * count
    for members, made in fed:
        for r, piece in zip(members, made.value):
            z_pieces[r] = piece
    back, forth = ring_scatter(z_pieces, count, add_rounded)
    z = z_pieces[0].astype(jnp.float32) + back.astype(jnp.float32) + forth.astype(jnp.float32)
    result = (hidden_next.astype(jnp.float32) + rms_scale(z, gains[3])).astype(jnp.bfloat16)
    return (result[None], fresh_out[None])


def solution(mesh):
    placed = (
        P("dp", "tensor", None),
        P("dp", None),
        P("dp", None),
        P("dp", None),
        P("dp", None),
        P("dp", "tensor", None),
        P("dp", "tensor", None),
        P(None, "dp", "tensor"),
        P("tensor", "dp"),
        P(None, "dp", "tensor"),
        P("tensor", "dp"),
        P(),
    )
    tensor, group = mesh.shape["tensor"], mesh.shape["dp"]

    def body(*arrays):
        columns = arrays[7].shape[2]
        whole_heads = columns % HEAD_DIM == 0 and tensor == 8 and group == 4
        return (ring_shards if whole_heads else shards)(*arrays)

    return jax.shard_map(
        body,
        mesh=mesh,
        in_specs=placed,
        out_specs=(P("dp", "tensor", None), P("dp", "tensor", None)),
        check_vma=False,
    )
```

```python
import functools
import math

import jax
import jax.numpy as jnp
from jax import lax
from jax.experimental import pallas as pl
from jax.experimental.pallas import tpu as pltpu
from jax.sharding import PartitionSpec as P

HEAD_DIM = 128
CH = 1024
NCH = 12
REQS = 3


THETA = 500000.0
EPSILON = 1e-06
NEGATIVE = -1e30
FLOOR = -1e28
MIB = 1024 * 1024


def token_meta(rows, order_row, length_row, offset_row):
    slot_index = rows // CH
    in_span = rows % CH
    ordinal = jnp.sum(
        jnp.where(
            slot_index[:, None] == jnp.arange(NCH, dtype=jnp.int32)[None, :], order_row[None, :], 0
        ),
        axis=1,
    )
    request_end = jnp.cumsum(length_row)
    request = jnp.sum((ordinal[:, None] >= request_end[None, :]).astype(jnp.int32), axis=1)
    request_pick = request[:, None] == jnp.arange(REQS, dtype=jnp.int32)[None, :]
    request_start = jnp.sum(jnp.where(request_pick, (request_end - length_row)[None, :], 0), axis=1)
    request_shift = jnp.sum(jnp.where(request_pick, offset_row[None, :], 0), axis=1)
    position = request_shift + (ordinal - request_start) * CH + in_span
    return (request, position, in_span)


def frequencies(index_float):
    return jnp.exp(index_float * (-2.0 * math.log(THETA) / HEAD_DIM))


def rope_full(values_in, position):
    row_count = values_in.shape[0]
    half_dim = HEAD_DIM // 2
    split = values_in.reshape(row_count, -1, HEAD_DIM)
    angles = (
        position.astype(jnp.float32)[:, None]
        * frequencies(jnp.arange(half_dim, dtype=jnp.int32).astype(jnp.float32))[None, :]
    )
    cosine = jnp.cos(angles)[:, None, :]
    sine = jnp.sin(angles)[:, None, :]
    first = split[..., :half_dim]
    second = split[..., half_dim:]
    turned = jnp.concatenate(
        [first * cosine - second * sine, second * cosine + first * sine], axis=-1
    )
    return turned.reshape(row_count, -1)


def rms_scale(values_in, gain):
    return (
        values_in
        * lax.rsqrt(jnp.mean(values_in * values_in, axis=-1, keepdims=True) + EPSILON)
        * gain
    )


def shards(
    hidden_sel,
    picked,
    order,
    lengths,
    offsets,
    cache_keys,
    cache_values,
    w_qkv,
    w_out,
    w_gate_up,
    w_down,
    gains,
):
    hidden = hidden_sel[0]
    picked_row = picked[0]
    order_row = order[0]
    length_row = lengths[0]
    offset_row = offsets[0]
    keys_local = cache_keys[0]
    values_local = cache_values[0]
    lane_count = lax.axis_size("tensor")
    lane_index = lax.axis_index("tensor")
    sel_dev = hidden.shape[0]
    sel_all = sel_dev * lane_count
    ctx_dev = keys_local.shape[0]
    model_width = hidden.shape[1]
    head_count = model_width // HEAD_DIM
    qkv_full, out_full = (
        lax.all_gather(w_qkv, "dp", axis=1, tiled=True),
        lax.all_gather(w_out, "dp", axis=1, tiled=True),
    )
    query_request, query_position, _ = token_meta(picked_row, order_row, length_row, offset_row)
    cache_rows = lane_index * ctx_dev + jnp.arange(ctx_dev, dtype=jnp.int32)
    cache_request, cache_position, cache_local = token_meta(
        cache_rows, order_row, length_row, offset_row
    )
    chosen = jnp.any(picked_row[:, None] == cache_rows[None, :], axis=0)
    fresh_request = lax.dynamic_slice_in_dim(query_request, lane_index * sel_dev, sel_dev)
    fresh_position = lax.dynamic_slice_in_dim(query_position, lane_index * sel_dev, sel_dev)
    projected = jnp.einsum(
        "nd,kdc->knc",
        lax.all_gather(hidden, "tensor", axis=0, tiled=True),
        qkv_full,
        preferred_element_type=jnp.float32,
    )
    own_rows = lax.all_to_all(
        projected.astype(jnp.bfloat16), "tensor", split_axis=1, concat_axis=2, tiled=True
    ).astype(projected.dtype)
    query_tok = rope_full(rms_scale(own_rows[0], gains[0]), fresh_position).astype(jnp.bfloat16)
    key_fresh = rope_full(rms_scale(own_rows[1], gains[1]), fresh_position).astype(jnp.bfloat16)
    value_fresh = own_rows[2].astype(jnp.bfloat16)
    queries = lax.all_gather(query_tok, "tensor", axis=0, tiled=True)
    turned_keys = rope_full(keys_local.astype(jnp.float32), cache_position - cache_local).astype(
        jnp.bfloat16
    )
    all_keys = jnp.concatenate([turned_keys, key_fresh], axis=0).reshape(-1, head_count, HEAD_DIM)
    all_values = jnp.concatenate([values_local, value_fresh], axis=0).reshape(
        -1, head_count, HEAD_DIM
    )
    key_request = jnp.concatenate([cache_request, fresh_request])
    key_position = jnp.concatenate([cache_position, fresh_position])
    key_live = jnp.concatenate([jnp.logical_not(chosen), jnp.ones((sel_dev,), bool)])
    block_rows = min(512, sel_all)
    block_count = sel_all // block_rows

    def attend(operands):
        query_block, block_request, block_position = operands
        scores = jnp.einsum(
            "qhd,khd->hqk",
            query_block.reshape(block_rows, head_count, HEAD_DIM),
            all_keys,
            preferred_element_type=jnp.float32,
        ) * HEAD_DIM ** (-0.5)
        usable = (
            (block_request[:, None] == key_request[None, :])
            & (key_position[None, :] <= block_position[:, None])
            & key_live[None, :]
        )
        masked = jnp.where(usable[None], scores, NEGATIVE)
        local_max = jnp.max(masked, axis=2)
        weights = jnp.where(usable[None], jnp.exp(masked - local_max[:, :, None]), 0.0)
        totals = jnp.sum(weights, axis=2)
        mixed = jnp.einsum(
            "hqk,khd->qhd",
            weights.astype(jnp.bfloat16),
            all_values,
            preferred_element_type=jnp.float32,
        )
        return (mixed.reshape(block_rows, model_width), local_max.T, totals.T)

    partial_out, local_max, totals = lax.map(
        attend,
        (
            queries.reshape(block_count, block_rows, model_width),
            query_request.reshape(block_count, block_rows),
            query_position.reshape(block_count, block_rows),
        ),
    )
    partial_out = partial_out.reshape(sel_all, model_width)
    local_max = local_max.reshape(sel_all, head_count)
    totals = totals.reshape(sel_all, head_count)
    row_max = lax.pmax(local_max.astype(jnp.bfloat16), "tensor").astype(local_max.dtype)
    factor = jnp.exp(local_max - row_max)
    scaled_out = (partial_out.reshape(sel_all, head_count, HEAD_DIM) * factor[:, :, None]).reshape(
        sel_all, model_width
    )
    scaled_total = totals * factor
    summed = lax.psum_scatter(
        scaled_out.astype(jnp.bfloat16), "tensor", scatter_dimension=0, tiled=True
    ).astype(jnp.float32)
    weight_sum = lax.psum_scatter(
        scaled_total.astype(jnp.bfloat16), "tensor", scatter_dimension=0, tiled=True
    ).astype(jnp.float32)
    attn_rows = (
        (summed.reshape(sel_dev, head_count, HEAD_DIM) / weight_sum[:, :, None])
        .reshape(sel_dev, model_width)
        .astype(jnp.bfloat16)
    )
    attn_cols = lax.all_to_all(attn_rows, "tensor", split_axis=1, concat_axis=0, tiled=True)
    attn_proj = lax.psum_scatter(
        jnp.dot(attn_cols, out_full, preferred_element_type=jnp.float32).astype(jnp.bfloat16),
        "tensor",
        scatter_dimension=0,
        tiled=True,
    ).astype(jnp.float32)
    hidden_next = (hidden.astype(jnp.float32) + rms_scale(attn_proj, gains[2])).astype(jnp.bfloat16)
    gate_full, down_full = (
        lax.all_gather(w_gate_up, "dp", axis=1, tiled=True),
        lax.all_gather(w_down, "dp", axis=1, tiled=True),
    )
    rows_piece = lax.all_gather(hidden_next, "tensor", axis=0, tiled=True)
    gate_part = jnp.dot(rows_piece, gate_full[0], preferred_element_type=jnp.float32)
    up_part = jnp.dot(rows_piece, gate_full[1], preferred_element_type=jnp.float32)
    activated = (jax.nn.silu(gate_part) * up_part).astype(jnp.bfloat16)
    mlp_out = lax.psum_scatter(
        jnp.dot(activated, down_full, preferred_element_type=jnp.float32).astype(jnp.bfloat16),
        "tensor",
        scatter_dimension=0,
        tiled=True,
    ).astype(jnp.float32)
    result = (hidden_next.astype(jnp.float32) + rms_scale(mlp_out, gains[3])).astype(jnp.bfloat16)
    return (result[None], key_fresh[None])


def lane_at(place, count):
    place = (place + count) % count
    return jnp.where(place < count // 2, 2 * place, 2 * (count - place) - 1)


def lane_back(distance, count):
    lane = lax.axis_index("tensor")
    place = jnp.where(lane % 2 == 0, lane // 2, count - (lane + 1) // 2)
    return lane_at(place - distance, count)


def ring_steps(count, shift):
    around = list(range(0, count, 2)) + list(range(count - 1, 0, -2))
    return [(around[i], around[(i + shift) % count]) for i in range(count)]


def ring_gather(block, count, work=None):
    blocks = [block] + [None] * (count - 1)
    forth = back = block
    work = work or (lambda step, blocks: None)
    made = None
    for step in range(1, count // 2 + 1):
        if made is not None:
            (forth, back), kept = lax.optimization_barrier(((forth, back), made.value))
            made.value = kept
        forth = lax.ppermute(forth, "tensor", ring_steps(count, 1))
        blocks[step] = forth
        if step < count - step:
            back = lax.ppermute(back, "tensor", ring_steps(count, -1))
            blocks[count - step] = back
        made = work(step - 1, blocks)
    work(count // 2, blocks)
    return blocks


class Made:
    def __init__(self, value):
        self.value = value


def ring_scatter(pieces, count, merge, more=None):
    half = count // 2
    back, forth = pieces[half], pieces[half + 1]
    arrived = None
    for step in range(1, half + 1):
        if step < half:
            forth = lax.ppermute(forth, "tensor", ring_steps(count, 1))
        back = lax.ppermute(back, "tensor", ring_steps(count, -1))
        if more is not None:
            more(step, arrived)
        arrived = back
        if step < half:
            back = merge(back, pieces[half - step])
        if step < half - 1:
            forth = merge(forth, pieces[half + 1 + step])
    return back, forth


def add_rounded(left, right):
    return (left.astype(jnp.float32) + right.astype(jnp.float32)).astype(jnp.bfloat16)


def dp_whole(weight, axis=1):
    return lax.all_gather(weight, "dp", axis=axis, tiled=True)


def upright(row):
    wide = jnp.broadcast_to(row.astype(jnp.float32), (HEAD_DIM, row.shape[1]))
    return wide.T


def prepare_kernel(
    order_ref, lengths_ref, offsets_ref, picked_ref, bias_ref, fresh_ref, angles_ref, piece_ref
):
    lane = lax.axis_index("tensor")
    ends = [lengths_ref[0, 0]]
    for request in range(1, REQS):
        ends.append(ends[-1] + lengths_ref[0, request])
    starts = [ends[request] - lengths_ref[0, request] for request in range(REQS)]

    def placed(ordinal):
        start = jnp.where(ordinal >= ends[0], starts[1], starts[0])
        shift = jnp.where(ordinal >= ends[0], offsets_ref[0, 1], offsets_ref[0, 0])
        for request in range(2, REQS):
            start = jnp.where(ordinal >= ends[request - 1], starts[request], start)
            shift = jnp.where(ordinal >= ends[request - 1], offsets_ref[0, request], shift)
        return start, shift

    picked = picked_ref[...]
    slot, local = picked // CH, picked % CH
    ordinal = jnp.zeros_like(picked)
    for index in range(NCH):
        ordinal = jnp.where(slot == index, order_ref[0, index], ordinal)
    start, shift = placed(ordinal)
    line, line_start = ordinal * CH + local, start * CH
    position = shift + (ordinal - start) * CH + local

    at = lax.broadcasted_iota(jnp.int32, (1, HEAD_DIM), 1) % (HEAD_DIM // 2)
    speed = frequencies(at.astype(jnp.float32))
    angles_ref[...] = upright(position) * speed
    line_column = upright(line)[:, :1].astype(jnp.int32)

    def bias_of(key_line):
        allowed = (key_line >= line_start) & (key_line <= line)
        return jnp.where(allowed, 0.0, NEGATIVE)

    fresh_ref[...] = bias_of(line_column).astype(jnp.bfloat16)
    rows = bias_ref.shape[0]
    piece = math.gcd(rows, CH)
    shifts = jnp.zeros((8, HEAD_DIM), jnp.float32)
    piece_at = lax.broadcasted_iota(jnp.int32, (8, HEAD_DIM), 0)
    for index in range(rows // piece):
        first = lane * rows + index * piece
        piece_slot = first // CH
        piece_ordinal = order_ref[0, piece_slot]
        piece_start, piece_shift = placed(piece_ordinal)
        moved = (piece_shift + (piece_ordinal - piece_start) * CH).astype(jnp.float32)
        shifts = jnp.where(piece_at == index, moved, shifts)
        row = first + lax.broadcasted_iota(jnp.int32, (piece, 1), 0)
        chosen = jnp.max(jnp.where(row == picked, 1.0, 0.0), axis=1, keepdims=True) > 0.5
        key_line = jnp.where(chosen, -1, piece_ordinal * CH + row % CH)
        bias_ref[index * piece : (index + 1) * piece, :] = bias_of(key_line).astype(jnp.bfloat16)
    piece_ref[...] = shifts * speed


def prepare(order, lengths, offsets, picked, ctx_dev):
    queries = picked.shape[1]
    smem = pl.BlockSpec(memory_space=pltpu.SMEM)
    vmem = pl.BlockSpec(memory_space=pltpu.VMEM)
    return pl.pallas_call(
        prepare_kernel,
        in_specs=[smem, smem, smem, vmem],
        out_specs=[vmem] * 4,
        out_shape=[
            jax.ShapeDtypeStruct((ctx_dev, queries), jnp.bfloat16),
            jax.ShapeDtypeStruct((queries, queries), jnp.bfloat16),
            jax.ShapeDtypeStruct((queries, HEAD_DIM), jnp.float32),
            jax.ShapeDtypeStruct((8, HEAD_DIM), jnp.float32),
        ],
        compiler_params=pltpu.CompilerParams(vmem_limit_bytes=57 * MIB),
        cost_estimate=pl.CostEstimate(
            flops=8 * ctx_dev * queries, bytes_accessed=4 * ctx_dev * queries, transcendentals=0
        ),
        name="prepare",
    )(order, lengths, offsets, picked)


def turn_kernel(first, piece, cos_ref, sin_ref, keys_ref, out_ref, buffer, sems):
    parts, rows, width = buffer.shape
    loads, stores = [], []
    for part in range(parts):
        loads.append(
            pltpu.make_async_copy(
                keys_ref.at[pl.ds(first + part * rows, rows), :], buffer.at[part], sems.at[0, part]
            )
        )
        stores.append(
            pltpu.make_async_copy(
                buffer.at[part], out_ref.at[pl.ds(part * rows, rows), :], sems.at[1, part]
            )
        )
        loads[part].start()
    for part in range(parts):
        at = (first + part * rows) // piece
        cosine, sine = cos_ref[at : at + 1, :], sin_ref[at : at + 1, :]
        loads[part].wait()
        for head in range(width // HEAD_DIM):
            cols = slice(head * HEAD_DIM, (head + 1) * HEAD_DIM)
            held = buffer[part, :, cols].astype(jnp.float32)
            turned = held * cosine + pltpu.roll(held, HEAD_DIM // 2, 1) * sine
            buffer[part, :, cols] = turned.astype(jnp.bfloat16)
        stores[part].start()
    for part in range(parts):
        stores[part].wait()


def turn_keys(first, rows, piece, keys, cosine, sine):
    width = keys.shape[1]
    per = math.gcd(math.gcd(rows, piece), 128)
    vmem = pl.BlockSpec(memory_space=pltpu.VMEM)
    whole = pl.BlockSpec(memory_space=pltpu.HBM)
    return pl.pallas_call(
        functools.partial(turn_kernel, first, piece),
        in_specs=[vmem, vmem, whole],
        out_specs=whole,
        out_shape=jax.ShapeDtypeStruct((rows, width), jnp.bfloat16),
        scratch_shapes=[
            pltpu.VMEM((rows // per, per, width), jnp.bfloat16),
            pltpu.SemaphoreType.DMA((2, rows // per)),
        ],
        compiler_params=pltpu.CompilerParams(vmem_limit_bytes=57 * MIB),
        cost_estimate=pl.CostEstimate(
            flops=4 * rows * width, bytes_accessed=4 * rows * width, transcendentals=0
        ),
        name="turn_keys",
    )(cosine, sine, keys)


def project_kernel(distances, earlier, *refs):
    blocks = len(distances)
    hidden_refs, refs = refs[:blocks], refs[blocks:]
    (weight_ref, gain_ref, cos_ref, sin_ref), refs = refs[:4], refs[4:]
    before, refs = refs[: 4 * len(earlier)], refs[4 * len(earlier) :]
    last = bool(earlier)
    (q_ref, k_ref, v_ref), refs = refs[:3], refs[3:]
    all_sums, rows_ref = (refs[1], refs[0]) if last else refs
    sel_dev = hidden_refs[0].shape[0]
    count = cos_ref.shape[0] // sel_dev
    width = weight_ref.shape[2]
    lane = lax.axis_index("tensor")

    def token_rows(distance):
        at = lane_back(distance, count) * sel_dev
        return pl.ds(pl.multiple_of(at, sel_dev), sel_dev)

    for index in range(blocks):
        rows_ref[index * sel_dev : (index + 1) * sel_dev, :] = hidden_refs[index][...]

    def project(kind):
        return jnp.dot(rows_ref[...], weight_ref[kind], preferred_element_type=jnp.float32)

    own = pl.ds(pl.multiple_of(lane * width, width), width)
    turned, squares = [], []
    tables = [
        jnp.concatenate([table[token_rows(d), :] for d in distances], axis=0)
        for table in (cos_ref, sin_ref)
    ]
    for kind in (0, 1):
        raw = project(kind)
        squares.append(jnp.sum(raw * raw, axis=1, keepdims=True))
        raw = raw * gain_ref[kind : kind + 1, own]
        turned.append([])
        for head in range(width // HEAD_DIM):
            part = raw[:, head * HEAD_DIM : (head + 1) * HEAD_DIM]
            turned[kind].append(part * tables[0] + pltpu.roll(part, HEAD_DIM // 2, 1) * tables[1])
    values = project(2)
    at = lax.broadcasted_iota(jnp.int32, (blocks * sel_dev, HEAD_DIM), 1)
    sums = jnp.where(at < HEAD_DIM // 2, squares[0], squares[1])
    for index, distance in enumerate(distances):
        rows = slice(index * sel_dev, (index + 1) * sel_dev)
        to = token_rows(distance) if last else rows
        for head in range(width // HEAD_DIM):
            cols = slice(head * HEAD_DIM, (head + 1) * HEAD_DIM)
            q_ref[to, cols] = turned[0][head][rows].astype(jnp.bfloat16)
            k_ref[to, cols] = turned[1][head][rows]
        v_ref[to, :] = values[rows].astype(jnp.bfloat16)
        all_sums[to, :] = sums[rows]
    for call, members in enumerate(earlier):
        for index, distance in enumerate(members):
            rows = slice(index * sel_dev, (index + 1) * sel_dev)
            to = token_rows(distance)
            for source, target in zip(before[4 * call : 4 * call + 4], (q_ref, k_ref, v_ref, all_sums)):
                target[to, :] = source[rows, :]
    if last:
        across = all_sums[...].T
        row = lax.broadcasted_iota(jnp.int32, (16, width), 0)
        tail = jnp.zeros((16, width), jnp.float32)
        at = 0
        for kind in (0, 1):
            line = across[kind * (HEAD_DIM // 2) : kind * (HEAD_DIM // 2) + 1]
            upper = line.astype(jnp.bfloat16).astype(jnp.float32)
            for part in (upper, line - upper):
                for start in range(0, line.shape[1], width):
                    tail = jnp.where(row == at, part[:, start : start + width], tail)
                    at += 1
        q_ref[line.shape[1] :, :] = tail.astype(jnp.bfloat16)


def project(distances, blocks, weight, gains, cosine, sine, earlier=(), outputs=()):
    sel_dev, model_width = blocks[0].shape
    width = weight.shape[2]
    last = bool(earlier)
    queries = cosine.shape[0] if last else sel_dev * len(blocks)
    vmem = pl.BlockSpec(memory_space=pltpu.VMEM)
    out_shape = [
        jax.ShapeDtypeStruct((queries + (16 if last else 0), width), jnp.bfloat16),
        jax.ShapeDtypeStruct((queries, width), jnp.float32),
        jax.ShapeDtypeStruct((queries, width), jnp.bfloat16),
    ]
    scratch = [pltpu.VMEM((sel_dev * len(blocks), model_width), jnp.bfloat16)]
    if last:
        scratch.append(pltpu.VMEM((queries, HEAD_DIM), jnp.float32))
    else:
        out_shape.append(jax.ShapeDtypeStruct((queries, HEAD_DIM), jnp.float32))
    return pl.pallas_call(
        functools.partial(project_kernel, distances, earlier),
        in_specs=[vmem] * (len(blocks) + 4 + len(outputs)),
        out_specs=[vmem] * len(out_shape),
        out_shape=out_shape,
        scratch_shapes=scratch,
        compiler_params=pltpu.CompilerParams(vmem_limit_bytes=16 * MIB),
        cost_estimate=pl.CostEstimate(
            flops=6 * sel_dev * len(blocks) * width * model_width,
            bytes_accessed=6 * model_width * width,
            transcendentals=0,
        ),
        name="project",
    )(*blocks, weight, gains, cosine, sine, *outputs)


def scales_kernel(model_width, *refs):
    out_ref = refs[-1]
    queries = out_ref.shape[1]
    width = refs[0].shape[1]
    tail = sum(ref[queries:, :].astype(jnp.float32) for ref in refs[:-1])
    rows = queries // width
    for kind in (0, 1):
        for index in range(rows):
            upper = tail[2 * rows * kind + index : 2 * rows * kind + index + 1]
            lower = tail[2 * rows * kind + rows + index : 2 * rows * kind + rows + index + 1]
            scale = lax.rsqrt((upper + lower) / model_width + EPSILON)
            if kind == 0:
                scale = scale * (HEAD_DIM ** (-0.5) * math.log2(math.e))
            out_ref[kind : kind + 1, index * width : (index + 1) * width] = scale


def scales(blocks, model_width):
    rows, width = blocks[0].shape
    vmem = pl.BlockSpec(memory_space=pltpu.VMEM)
    return pl.pallas_call(
        functools.partial(scales_kernel, model_width),
        in_specs=[vmem] * len(blocks),
        out_specs=vmem,
        out_shape=jax.ShapeDtypeStruct((2, rows - 16), jnp.float32),
        compiler_params=pltpu.CompilerParams(vmem_limit_bytes=8 * MIB),
        cost_estimate=pl.CostEstimate(flops=rows, bytes_accessed=rows, transcendentals=rows),
        name="scales",
    )(*blocks)


def tail_rows(rows, wide):
    at = lax.broadcasted_iota(jnp.int32, (16, wide), 0)
    tail = jnp.zeros((16, wide), jnp.float32)
    for index, row in enumerate(rows):
        tail = jnp.where(at == index, row, tail)
    return tail.astype(jnp.bfloat16)


def attend_one(q_ref, key_refs, value_ref, columns, scale_ref, bias_ref, out_ref):
    width = q_ref.shape[1]
    queries = scale_ref.shape[1]
    scale = scale_ref[0:1, :]
    parts, start = [], 0
    for ref in key_refs:
        parts.append(slice(start, start + ref.shape[0]))
        start += ref.shape[0]
    raw = [
        [
            lax.dot_general(
                ref[:, cols],
                q_ref[:queries, head * HEAD_DIM : (head + 1) * HEAD_DIM],
                (((1,), (1,)), ((), ())),
                preferred_element_type=jnp.float32,
            )
            for ref in key_refs
        ]
        for head, cols in enumerate(columns)
    ]
    tops, totals = [], []
    for head, cols in enumerate(columns):
        scores = [
            part * scale + bias_ref[rows, :].astype(jnp.float32)
            for part, rows in zip(raw[head], parts)
        ]
        top = functools.reduce(
            jnp.maximum, [jnp.max(part, axis=0, keepdims=True) for part in scores]
        )
        top = jnp.maximum(top, FLOOR).astype(jnp.bfloat16).astype(jnp.float32)
        weights = [jnp.exp2(part - top) for part in scores]
        tops.append(top)
        totals.append(sum(jnp.sum(part, axis=0, keepdims=True) for part in weights))
        mixed = sum(
            lax.dot_general(
                value_ref[rows, cols],
                part.astype(jnp.bfloat16),
                (((0,), (0,)), ((), ())),
                preferred_element_type=jnp.float32,
            )
            for rows, part in zip(parts, weights)
        )
        out_ref[head * HEAD_DIM : (head + 1) * HEAD_DIM, :] = mixed.astype(jnp.bfloat16)
    out_ref[width : width + 16, :] = tail_rows(tops + totals, queries)


def fresh_kernel(scale_ref, bias_ref, q_ref, k_ref, v_ref, out_ref, keys_ref):
    columns = [
        slice(start, start + HEAD_DIM) for start in range(0, q_ref.shape[1], HEAD_DIM)
    ]
    scale = upright(scale_ref[1:2, :])
    for cols in columns:
        keys_ref[:, cols] = (k_ref[:, cols] * scale).astype(jnp.bfloat16)
    attend_one(q_ref, [keys_ref], v_ref, columns, scale_ref, bias_ref, out_ref)


def attend_kernel(distances, devices, scale_ref, bias_ref, *refs):
    count = len(distances)
    q_refs, kv_refs, out_refs = refs[:count], refs[count:-count], refs[-count:]
    width = q_refs[0].shape[1]
    for index, distance in enumerate(distances):
        lane = lane_back(distance, devices)
        columns = [
            pl.ds(pl.multiple_of(lane * width + start, HEAD_DIM), HEAD_DIM)
            for start in range(0, width, HEAD_DIM)
        ]
        attend_one(
            q_refs[index],
            kv_refs[:-1],
            kv_refs[-1],
            columns,
            scale_ref,
            bias_ref,
            out_refs[index],
        )


def attend_cost(count, queries, width, key_rows):
    return pl.CostEstimate(
        flops=4 * count * queries * width * key_rows,
        bytes_accessed=4 * count * width * key_rows,
        transcendentals=count * queries * key_rows * width // HEAD_DIM,
    )


def attend_fresh(query, keys, values, scale, bias):
    queries, width = values.shape
    vmem = pl.BlockSpec(memory_space=pltpu.VMEM)
    return pl.pallas_call(
        fresh_kernel,
        in_specs=[vmem] * 5,
        out_specs=vmem,
        out_shape=jax.ShapeDtypeStruct((width + 16, queries), jnp.bfloat16),
        scratch_shapes=[pltpu.VMEM((queries, width), jnp.bfloat16)],
        compiler_params=pltpu.CompilerParams(vmem_limit_bytes=16 * MIB),
        cost_estimate=attend_cost(1, queries, width, queries),
        name="attend_fresh",
    )(scale, bias, query, keys, values)


def attend(distances, devices, blocks, scale, keys, values, bias):
    count = len(blocks)
    width = blocks[0].shape[1]
    key_rows, queries = bias.shape
    vmem = pl.BlockSpec(memory_space=pltpu.VMEM)
    return pl.pallas_call(
        functools.partial(attend_kernel, distances, devices),
        in_specs=[vmem] * (3 + count + len(keys)),
        out_specs=[vmem] * count,
        out_shape=[jax.ShapeDtypeStruct((width + 16, queries), jnp.bfloat16)] * count,
        compiler_params=pltpu.CompilerParams(vmem_limit_bytes=28 * MIB),
        cost_estimate=attend_cost(count, queries, width, key_rows),
        name="attend",
    )(scale, bias, *blocks, *keys, values)


def merged(refs, width):
    heads = width // HEAD_DIM
    tails = [ref[width : width + 16, :].astype(jnp.float32) for ref in refs]
    mixed, tops, totals = [], [], []
    for head in range(heads):
        top = functools.reduce(jnp.maximum, [tail[head : head + 1] for tail in tails])
        factors = [jnp.exp2(tail[head : head + 1] - top) for tail in tails]
        cols = slice(head * HEAD_DIM, (head + 1) * HEAD_DIM)
        mixed.append(sum(ref[cols, :].astype(jnp.float32) * f for ref, f in zip(refs, factors)))
        totals.append(
            sum(tail[heads + head : heads + head + 1] * f for tail, f in zip(tails, factors))
        )
        tops.append(top)
    return mixed, tops, totals


def merge_kernel(left_ref, right_ref, out_ref):
    width = out_ref.shape[0] - 16
    mixed, tops, totals = merged([left_ref, right_ref], width)
    for head, part in enumerate(mixed):
        out_ref[head * HEAD_DIM : (head + 1) * HEAD_DIM, :] = part.astype(jnp.bfloat16)
    out_ref[width : width + 16, :] = tail_rows(tops + totals, out_ref.shape[1])


def merge_partials(left, right):
    vmem = pl.BlockSpec(memory_space=pltpu.VMEM)
    return pl.pallas_call(
        merge_kernel,
        in_specs=[vmem, vmem],
        out_specs=vmem,
        out_shape=jax.ShapeDtypeStruct(left.shape, jnp.bfloat16),
        compiler_params=pltpu.CompilerParams(vmem_limit_bytes=4 * MIB),
        cost_estimate=pl.CostEstimate(
            flops=3 * left.size, bytes_accessed=6 * left.size, transcendentals=0
        ),
        name="merge_partials",
    )(left, right)


def output_kernel(*refs):
    partial_refs, weight_ref, out_refs = refs[:4], refs[4], refs[5:-2]
    attn_ref, rows_ref = refs[-2:]
    width = attn_ref.shape[1]
    count, sel_dev = len(out_refs), out_refs[0].shape[0]
    mixed, _, totals = merged(partial_refs, width)
    for head, part in enumerate(mixed):
        cols = slice(head * HEAD_DIM, (head + 1) * HEAD_DIM)
        attn_ref[:, cols] = (part / totals[head]).T.astype(jnp.bfloat16)
    rows_ref[...] = jnp.dot(
        attn_ref[...], weight_ref[...], preferred_element_type=jnp.float32
    ).astype(jnp.bfloat16)
    for r in range(count):
        at = pl.multiple_of(lane_back(r, count) * sel_dev, sel_dev)
        out_refs[r][...] = rows_ref[pl.ds(at, sel_dev), :]


def output_rows(partials, weight, count):
    queries = partials[0].shape[1]
    width, model_width = weight.shape
    vmem = pl.BlockSpec(memory_space=pltpu.VMEM)
    return pl.pallas_call(
        output_kernel,
        in_specs=[vmem] * 5,
        out_specs=[vmem] * count,
        out_shape=[jax.ShapeDtypeStruct((queries // count, model_width), jnp.bfloat16)] * count,
        scratch_shapes=[
            pltpu.VMEM((queries, width), jnp.bfloat16),
            pltpu.VMEM((queries, model_width), jnp.bfloat16),
        ],
        compiler_params=pltpu.CompilerParams(vmem_limit_bytes=16 * MIB),
        cost_estimate=pl.CostEstimate(
            flops=2 * queries * width * model_width,
            bytes_accessed=2 * width * model_width + 2 * queries * model_width,
            transcendentals=0,
        ),
        name="output_rows",
    )(*partials, weight)


def feed_kernel(*refs):
    count = (len(refs) - 3) // 2
    row_refs, (up_ref, down_ref), out_refs = refs[:count], refs[count : count + 2], refs[count + 2 : -1]
    rows_ref = refs[-1]
    sel_dev, model_width = row_refs[0].shape
    units = up_ref.shape[2]
    per = math.gcd(units, 256)
    for r in range(count):
        rows_ref[r * sel_dev : (r + 1) * sel_dev, :] = row_refs[r][...]
    active = []
    for start in range(0, units, per):
        gate, up = [
            jnp.dot(
                rows_ref[...],
                up_ref[kind, :, start : start + per],
                preferred_element_type=jnp.float32,
            )
            for kind in (0, 1)
        ]
        active.append((gate * jax.nn.sigmoid(gate) * up).astype(jnp.bfloat16))
    active = jnp.concatenate(active, axis=1)
    wide = math.gcd(model_width, 512)
    for start in range(0, model_width, wide):
        cols = slice(start, start + wide)
        part = jnp.dot(active, down_ref[:, cols], preferred_element_type=jnp.float32)
        for r in range(count):
            out_refs[r][:, cols] = part[r * sel_dev : (r + 1) * sel_dev].astype(jnp.bfloat16)


def feed_forward(row_blocks, up_weight, down_weight):
    count = len(row_blocks)
    sel_dev, model_width = row_blocks[0].shape
    units = up_weight.shape[2]
    queries = count * sel_dev
    vmem = pl.BlockSpec(memory_space=pltpu.VMEM)
    return pl.pallas_call(
        feed_kernel,
        in_specs=[vmem] * (count + 2),
        out_specs=[vmem] * count,
        out_shape=[jax.ShapeDtypeStruct((sel_dev, model_width), jnp.bfloat16)] * count,
        scratch_shapes=[pltpu.VMEM((queries, model_width), jnp.bfloat16)],
        compiler_params=pltpu.CompilerParams(vmem_limit_bytes=16 * MIB),
        cost_estimate=pl.CostEstimate(
            flops=6 * queries * model_width * units,
            bytes_accessed=4 * queries * model_width,
            transcendentals=queries * units,
        ),
        name="feed_forward",
    )(*row_blocks, up_weight, down_weight)


def rotation_tables(angles):
    flip = jnp.where(jnp.arange(HEAD_DIM) < HEAD_DIM // 2, -1.0, 1.0)
    return jnp.cos(angles), jnp.sin(angles) * flip


def ring_shards(
    hidden_sel,
    picked,
    order,
    lengths,
    offsets,
    cache_keys,
    cache_values,
    w_qkv,
    w_out,
    w_gate_up,
    w_down,
    gains,
):
    hidden = hidden_sel[0]
    count = lax.axis_size("tensor")
    sel_dev, model_width = hidden.shape
    sel_all = sel_dev * count
    ctx_dev = cache_keys.shape[1]

    half = count // 2
    near = [0, 1, count - 1]
    middle = [r for r in range(count) if r not in near and r != half]

    qkv_full = dp_whole(w_qkv)
    piece = math.gcd(ctx_dev, CH)
    tables = []

    def early_work(step, blocks):
        if step != 0:
            return None
        masks = prepare(order, lengths, offsets, picked, ctx_dev)
        tables.append(Made((masks[0], masks[1], rotation_tables(masks[2]), masks[3])))
        return tables[0]

    hidden_blocks = ring_gather(hidden, count, early_work)
    bias_cache, bias_fresh, (cos_table, sin_table), piece_angles = tables[0].value
    w_out, w_gate_up, w_down, bias_cache = lax.optimization_barrier(
        (w_out, w_gate_up, w_down, bias_cache)
    )
    out_full, up_full, down_full = dp_whole(w_out), dp_whole(w_gate_up), dp_whole(w_down)
    outputs, calls = [], [near, middle]
    for members in calls:
        outputs += project(
            members, [hidden_blocks[r] for r in members], qkv_full, gains, cos_table, sin_table
        )
    q_sent, k_turned, v_own = project(
        [half],
        [hidden_blocks[half]],
        qkv_full,
        gains,
        cos_table,
        sin_table,
        earlier=calls,
        outputs=outputs,
    )

    q_sent, piece_angles, k_sent = lax.optimization_barrier(
        (q_sent, piece_angles, k_turned.astype(jnp.bfloat16))
    )
    cos_piece, sin_piece = rotation_tables(piece_angles)
    turned = []

    def turn_work(step, blocks):
        if step in (0, 1):
            rows = ctx_dev // 2
            made = Made(turn_keys(step * rows, rows, piece, cache_keys[0], cos_piece, sin_piece))
            turned.append(made)
            return made
        return None

    q_blocks = ring_gather(q_sent, count, turn_work)
    turned = [made.value for made in turned]
    k_sent, q_blocks[1] = lax.optimization_barrier((k_sent, q_blocks[1]))
    k_sent = k_sent.reshape(count, sel_dev, -1)
    owned = lax.all_to_all(k_sent, "tensor", split_axis=0, concat_axis=0, tiled=True)
    owned, q_blocks[half] = lax.optimization_barrier((owned, q_blocks[half]))
    scale = scales(q_blocks, model_width)

    partials = [None] * count
    fresh = []

    def attend_members(members, arrived):
        blocks = [q_blocks[r] for r in members]
        if arrived is not None:
            blocks, _ = lax.optimization_barrier((blocks, arrived))
        out = attend(members, count, blocks, scale, turned, cache_values[0], bias_cache)
        for r, made in zip(members, out):
            partials[r] = made

    def attend_more(step, arrived):
        if step < half:
            attend_members(sorted({half - step, half + 1 + step} - {count}), arrived)
        else:
            attend_members([0], arrived)
            fresh.append(attend_fresh(q_sent, k_turned, v_own, scale, bias_fresh))

    attend_members([half, half + 1], None)
    back, forth = ring_scatter(partials, count, merge_partials, attend_more)
    fresh = fresh[0]

    y_pieces = list(output_rows([partials[0], back, forth, fresh], out_full, count))
    owned, scale, y_pieces[1] = lax.optimization_barrier((owned, scale, y_pieces[1]))
    own_scale = lax.dynamic_slice_in_dim(scale[1], lax.axis_index("tensor") * sel_dev, sel_dev)
    fresh_out = owned.astype(jnp.float32) * own_scale[None, :, None]
    fresh_out = fresh_out.astype(jnp.bfloat16).transpose(1, 0, 2).reshape(sel_dev, model_width)
    back, forth = ring_scatter(y_pieces, count, add_rounded)
    y = y_pieces[0].astype(jnp.float32) + back.astype(jnp.float32) + forth.astype(jnp.float32)
    hidden_next = (hidden.astype(jnp.float32) + rms_scale(y, gains[2])).astype(jnp.bfloat16)

    fed = []

    def feed_work(step, blocks):
        members = {1: near, half - 1: middle, half: [half]}.get(step)
        if not members:
            return None
        rows = [blocks[r] for r in members]
        if step == half:
            rows, fed[-1][1].value = lax.optimization_barrier((rows, fed[-1][1].value))
        made = Made(feed_forward(rows, up_full, down_full))
        fed.append((members, made))
        return made

    ring_gather(hidden_next, count, feed_work)
    z_pieces = [None] * count
    for members, made in fed:
        for r, piece in zip(members, made.value):
            z_pieces[r] = piece
    back, forth = ring_scatter(z_pieces, count, add_rounded)
    z = z_pieces[0].astype(jnp.float32) + back.astype(jnp.float32) + forth.astype(jnp.float32)
    result = (hidden_next.astype(jnp.float32) + rms_scale(z, gains[3])).astype(jnp.bfloat16)
    return (result[None], fresh_out[None])


def solution(mesh):
    placed = (
        P("dp", "tensor", None),
        P("dp", None),
        P("dp", None),
        P("dp", None),
        P("dp", None),
        P("dp", "tensor", None),
        P("dp", "tensor", None),
        P(None, "dp", "tensor"),
        P("tensor", "dp"),
        P(None, "dp", "tensor"),
        P("tensor", "dp"),
        P(),
    )
    tensor, group = mesh.shape["tensor"], mesh.shape["dp"]

    def body(*arrays):
        columns = arrays[7].shape[2]
        whole_heads = columns % HEAD_DIM == 0 and tensor == 8 and group == 4
        return (ring_shards if whole_heads else shards)(*arrays)

    return jax.shard_map(
        body,
        mesh=mesh,
        in_specs=placed,
        out_specs=(P("dp", "tensor", None), P("dp", "tensor", None)),
        check_vma=False,
    )
```
